32 devices in a mesh: ctx: 16 (over z, y, core), head: 2 (over x).
Axes of the slice: x: 2, y: 2, z: 4, core: 2. Of those that a mesh axis runs over, the one named last changes fastest.
Arguments:
- queries: bfloat16 [1, 16384, 256], P(None, ('ctx', 'head')), may hold values from -150 to 150
- keys: bfloat16 [1, 16384, 256], P(None, ('ctx', 'head')), may hold values from -32 to 32
- values: bfloat16 [1, 16384, 256], P(None, ('ctx', 'head')), may hold values from -6 to 6
- rates: float32 [1, 2, 16384], P(None, 'head', 'ctx'), may hold values from 0.0002 to 0.004
- tail_keys: bfloat16 [8192, 256], P('ctx', 'head'), may hold values from -6 to 6
- tail_values: bfloat16 [8192, 256], P('ctx', 'head'), may hold values from -6 to 6
- state_in_gu: float32 [16, 2, 2, 128, 256], P('ctx', 'head'), may hold values from -0.5 to 0.5
- state_in_down: float32 [16, 2, 256, 128], P('ctx', 'head'), may hold values from -0.375 to 0.375
- fresh_gu: float32 [2, 2, 128, 256], P('head'), may hold values from -0.5 to 0.5
- fresh_down: float32 [2, 256, 128], P('head'), may hold values from -0.375 to 0.375
- out_gain: float32 [256], P('head'), may hold values from 0.1 to 1.9
- seq_ids: int32 [16, 2], replicated, may hold values from 0 to 31, as said below
- live_lengths: int32 [16, 1], replicated, may hold values from 1 to 1024, as said below
Outputs:
- mixed: bfloat16 [1, 16384, 256], P(None, ('ctx', 'head'))
- state_out_gu: float32 [16, 2, 2, 128, 256], P('ctx', 'head')
- state_out_down: float32 [16, 2, 256, 128], P('ctx', 'head')
The draws below stay inside these ranges and needn't reach their ends.
Inputs may be any that keep to these rules, and one draw needn't show every extreme that they name: `seq_ids`: block (c, t + 1) continues the sequence of block ((c - 1) mod 16, t) exactly when their numbers agree, else it begins a new sequence; different sequences have different numbers. `live_lengths`: only a block whose successor (device c + 1 mod 16, step t + 1) begins a new sequence is shorter than 1024; its live tokens are the first ones.
All inputs are finite; a program needn't handle non-finite values.
Results may differ from the reference program's by a relative error of at most 0.0028.
Values may be sent and summed in bfloat16 or wider, within the bound.
No kernel may reach another device: no remote copies, remote signals or barrier semaphores. Data moves between devices by JAX's collectives and lax.ppermute only.
A program may use at most 64 MiB of HBM per device.

```python
import math
import jax
import jax.numpy as jnp
from jax import lax

HD = 128
HID = 256
BLOCK = 1024
WIN = 512
STEPS = 1
HEADS = 2
FEATURES = 256
TOK_STEP = 16384
N_CTX = 16


def paired_draw(key):
    inner = jax.random.fold_in(key, 11)
    streams = jax.random.split(inner, 6)
    shape = (STEPS, TOK_STEP, HEADS, HD)
    base_query = jnp.clip(jax.random.normal(streams[0], shape, jnp.float32), -4.0, 4.0)
    base_key = jnp.clip(jax.random.normal(streams[1], shape, jnp.float32), -4.0, 4.0)
    row_query = jnp.exp(jax.random.uniform(streams[2], (STEPS, TOK_STEP, HEADS, 1), jnp.float32, math.log(0.32), math.log(3.2)))
    col_query = jnp.exp(jax.random.uniform(streams[3], (HEADS, HD), jnp.float32, math.log(0.6), math.log(1.8)))
    row_key = jnp.exp(jax.random.uniform(streams[4], (STEPS, TOK_STEP, HEADS, 1), jnp.float32, math.log(0.32), math.log(3.2)))
    col_key = jnp.exp(jax.random.uniform(streams[5], (HEADS, HD), jnp.float32, math.log(0.6), math.log(1.8)))
    query_draw = base_query * row_query * col_query
    key_draw = base_key * row_key * col_key
    query_draw = query_draw.reshape(STEPS, TOK_STEP, HEADS * HD).astype(jnp.bfloat16)
    key_draw = key_draw.reshape(STEPS, TOK_STEP, HEADS * HD).astype(jnp.bfloat16)
    return (query_draw, key_draw)


def draw_queries(key, part):
    return paired_draw(key)[0]


def draw_keys(key, part):
    return paired_draw(key)[1]


def chain_layout(key):
    inner = jax.random.fold_in(key, 23)
    streams = jax.random.split(inner, 2)
    ctx_count = TOK_STEP // BLOCK
    starts = jax.random.randint(streams[0], (ctx_count, STEPS), 0, 10) < 3
    starts = starts.at[2, 0].set(True).at[1, 0].set(False).at[ctx_count - 1, STEPS - 1].set(True)
    for column in range(STEPS):
        starts = starts.at[(ctx_count - column) % ctx_count, column].set(False)
    column_ids = jnp.arange(1, STEPS + 1, dtype=jnp.int32)
    marks = jnp.where(starts, column_ids[None, :], 0)
    recent = lax.cummax(marks, axis=1)
    recent = jnp.concatenate([jnp.zeros((ctx_count, 1), jnp.int32), recent], axis=1)
    chain_ids = jnp.arange(ctx_count, dtype=jnp.int32)[:, None] * (STEPS + 1) + recent
    is_last = jnp.concatenate([starts[:, 1:], jnp.zeros((ctx_count, 1), bool)], axis=1)
    ragged = jax.random.randint(streams[1], (ctx_count, STEPS), 1, BLOCK + 1)
    chain_lengths = jnp.where(is_last, ragged, BLOCK)
    seq_columns = [jnp.roll(chain_ids[:, column], column - 1) for column in range(STEPS + 1)]
    length_columns = [jnp.roll(chain_lengths[:, column], column) for column in range(STEPS)]
    return (jnp.stack(seq_columns, axis=1).astype(jnp.int32), jnp.stack(length_columns, axis=1).astype(jnp.int32))


def draw_seq_ids(key, part):
    return chain_layout(key)[0]


def draw_live_lengths(key, part):
    return chain_layout(key)[1]


def levels(rng, shape, cuts, least, top_value):
    def one(dim, shards_of):
        draws = jax.random.uniform(jax.random.fold_in(jax.random.fold_in(rng, 6), dim), (shards_of,), jnp.float32, least / len(cuts), top_value / len(cuts))
        return jnp.repeat(jnp.exp(draws), shape[dim] // shards_of).reshape((-1,) + (1,) * (len(shape) - dim - 1))

    loudness = one(*cuts[0])
    for cut in cuts[1:]:
        loudness = loudness * one(*cut)
    return loudness


def gaussian(key, extent, spread, reach, shards=(), kind=jnp.bfloat16):
    values = spread * jax.random.normal(key, extent, jnp.float32)
    if shards:
        values = values * levels(key, extent, shards, -0.22, 0.18)
    return jnp.clip(values, -reach, reach).astype(kind)


def setup_inputs(seed: int = 0) -> dict:
    key_of = jax.random.split(jax.random.key(seed), 14)
    queries = draw_queries(jax.random.fold_in(key_of[13], 71), 0)
    keys = draw_keys(jax.random.fold_in(key_of[13], 71), 0)
    values = gaussian(key_of[2], (STEPS, TOK_STEP, FEATURES), 1.0, 6.0, ((1, 32),))
    rates = jnp.clip(jnp.exp(math.log(0.004) - 2.9957323 * jax.random.uniform(key_of[3], (STEPS, HEADS, TOK_STEP), jnp.float32) ** levels(key_of[3], (STEPS, HEADS, TOK_STEP), ((1, 2), (2, 16)), -0.2, 0.2)), 0.0002, 0.004)
    tail_keys = gaussian(key_of[4], (N_CTX * WIN, FEATURES), 1.0, 6.0, ((0, 16), (1, 2)))
    tail_values = gaussian(key_of[5], (N_CTX * WIN, FEATURES), 1.0, 6.0, ((0, 16), (1, 2)))
    state_in_gu = gaussian(key_of[6], (N_CTX, HEADS, 2, HD, HID), HD ** -0.5, 0.5, ((0, 16), (1, 2)), jnp.float32)
    state_in_down = gaussian(key_of[7], (N_CTX, HEADS, HID, HD), HID ** -0.5, 0.375, ((0, 16), (1, 2)), jnp.float32)
    fresh_gu = gaussian(key_of[8], (HEADS, 2, HD, HID), HD ** -0.5, 0.5, ((0, 2),), jnp.float32)
    fresh_down = gaussian(key_of[9], (HEADS, HID, HD), HID ** -0.5, 0.375, ((0, 2),), jnp.float32)
    out_gain = jnp.clip(1.0 + 0.18 * jax.random.normal(key_of[10], (FEATURES,), jnp.float32), 0.1, 1.9)
    seq_ids = draw_seq_ids(jax.random.fold_in(key_of[13], 71), 0)
    live_lengths = draw_live_lengths(jax.random.fold_in(key_of[13], 71), 0)
    return {"queries": queries, "keys": keys, "values": values, "rates": rates, "tail_keys": tail_keys, "tail_values": tail_values, "state_in_gu": state_in_gu, "state_in_down": state_in_down, "fresh_gu": fresh_gu, "fresh_down": fresh_down, "out_gain": out_gain, "seq_ids": seq_ids, "live_lengths": live_lengths}


epsilon = 1e-06

def highest(left, right):
    return jnp.dot(left, right, precision=lax.Precision.HIGHEST)

def rms_rows(matrix):
    return matrix / jnp.sqrt(lax.optimization_barrier(jnp.mean(matrix * matrix, axis=-1, keepdims=True)) + epsilon)

def renormed(old_weight, new_weight):
    old_scale = jnp.sqrt(lax.optimization_barrier(jnp.mean(old_weight * old_weight, axis=0, keepdims=True)) + epsilon)
    new_scale = jnp.sqrt(lax.optimization_barrier(jnp.mean(new_weight * new_weight, axis=0, keepdims=True)) + epsilon)
    return new_weight * (old_scale / new_scale)

def fast_block(block_q, block_k, block_v, rate_row, prior_keys, prior_values, gate_up, down_proj, fresh_pair, fresh_proj, head_gain, length, linked):
    block_len = block_q.shape[0]
    window = prior_keys.shape[0]
    head_dim = block_q.shape[1]
    gate_up = jnp.where(linked, gate_up, fresh_pair)
    down_proj = jnp.where(linked, down_proj, fresh_proj)
    joined_keys = jnp.concatenate([prior_keys, block_k], axis=0)
    joined_values = jnp.concatenate([prior_values, block_v], axis=0)
    row_index = jnp.arange(window)[:, None]
    col_index = jnp.arange(2 * window)[None, :]
    pieces = []
    for offset in range(0, block_len, window):
        query_pos = offset + row_index
        key_pos = offset - window + col_index
        allowed = (key_pos <= query_pos) & (key_pos > query_pos - window) & ((key_pos < length) | (key_pos == query_pos)) & ((key_pos >= 0) | linked)
        scores = jnp.dot(block_q[offset:offset + window], joined_keys[offset:offset + 2 * window].T, preferred_element_type=jnp.float32) * (1.0 / math.sqrt(head_dim))
        scores = jnp.where(allowed, scores, -1e+30)
        largest = lax.optimization_barrier(jnp.max(scores, axis=-1, keepdims=True))
        exponent = jnp.exp(scores - largest)
        weights = (exponent / lax.optimization_barrier(jnp.sum(exponent, axis=-1, keepdims=True))).astype(jnp.bfloat16)
        pieces.append(jnp.dot(weights, joined_values[offset:offset + 2 * window], preferred_element_type=jnp.float32))
    attended = jnp.concatenate(pieces, axis=0)
    query_unit = rms_rows(block_q.astype(jnp.float32))
    key_unit = rms_rows(block_k.astype(jnp.float32))
    w_gate = gate_up[0]
    w_up = gate_up[1]
    fast_out = highest(jax.nn.silu(highest(query_unit, w_gate)) * highest(query_unit, w_up), down_proj)
    live_rows = (jnp.arange(block_len) < length).astype(jnp.float32)[:, None]
    mixed = ((attended + rms_rows(fast_out) * head_gain) * live_rows).astype(jnp.bfloat16)
    key_gate = highest(key_unit, w_gate)
    key_up = highest(key_unit, w_up)
    gate_sigmoid = jax.nn.sigmoid(key_gate)
    gate_act = key_gate * gate_sigmoid
    out_grad = -(rate_row[:, None] * live_rows) * block_v.astype(jnp.float32)
    grad_down = highest((gate_act * key_up).T, out_grad)
    hidden_grad = highest(out_grad, down_proj.T)
    grad_up = highest(key_unit.T, hidden_grad * gate_act)
    grad_gate = highest(key_unit.T, hidden_grad * key_up * gate_sigmoid * (1.0 + key_gate * (1.0 - gate_sigmoid)))
    new_pair = jnp.stack([renormed(w_gate, w_gate - grad_gate), renormed(w_up, w_up - grad_up)])
    new_down = renormed(down_proj, down_proj - grad_down)
    return (mixed, new_pair, new_down)

def reference(queries, keys, values, rates, tail_keys, tail_values, state_in_gu, state_in_down, fresh_gu, fresh_down, out_gain, seq_ids, live_lengths):

    def by_head(array):
        return array.reshape(STEPS, N_CTX, BLOCK, HEADS, HD).transpose(0, 1, 3, 2, 4)
    query_heads = by_head(queries)
    key_heads = by_head(keys)
    value_heads = by_head(values)
    rate_heads = rates.reshape(STEPS, HEADS, N_CTX, BLOCK).transpose(0, 2, 1, 3)
    tail_key_heads = tail_keys.reshape(N_CTX, WIN, HEADS, HD).transpose(0, 2, 1, 3)
    tail_value_heads = tail_values.reshape(N_CTX, WIN, HEADS, HD).transpose(0, 2, 1, 3)
    head_gains = out_gain.reshape(HEADS, HD)
    apply_heads = jax.vmap(fast_block, in_axes=(0, 0, 0, 0, 0, 0, 0, 0, 0, 0, 0, None, None))

    def per_device(packed):
        return apply_heads(packed[0], packed[1], packed[2], packed[3], packed[4], packed[5], packed[6], packed[7], fresh_gu, fresh_down, head_gains, packed[8], packed[9])
    gate_up = state_in_gu
    down_proj = state_in_down
    results = []
    for wave_step in range(STEPS):
        if wave_step == 0:
            source_keys = tail_key_heads
            source_values = tail_value_heads
        else:
            source_keys = key_heads[wave_step - 1][:, :, BLOCK - WIN:]
            source_values = value_heads[wave_step - 1][:, :, BLOCK - WIN:]
        prior_keys = jnp.roll(source_keys, 1, axis=0)
        prior_values = jnp.roll(source_values, 1, axis=0)
        moved_pair = jnp.roll(gate_up, 1, axis=0)
        moved_proj = jnp.roll(down_proj, 1, axis=0)
        linked = seq_ids[:, wave_step + 1] == jnp.roll(seq_ids[:, wave_step], 1)
        lengths = live_lengths[:, wave_step]
        mixed_step, gate_up, down_proj = lax.map(per_device, (query_heads[wave_step], key_heads[wave_step], value_heads[wave_step], rate_heads[wave_step], prior_keys, prior_values, moved_pair, moved_proj, lengths, linked))
        results.append(mixed_step)
    mixed = jnp.stack(results).transpose(0, 1, 3, 2, 4).reshape(STEPS, N_CTX * BLOCK, HEADS * HD)
    return (mixed, gate_up, down_proj)
```

```python
import functools
import math

import jax
import jax.numpy as jnp
from jax import lax
from jax.experimental import pallas as pl
from jax.experimental.pallas import tpu as pltpu
from jax.sharding import PartitionSpec as P

epsilon = 1e-06
masked = -1e30
f32 = jnp.float32
bf16 = jnp.bfloat16

VMEM = pltpu.VMEM
in_vmem = pl.BlockSpec(memory_space=pltpu.VMEM)
in_smem = pl.BlockSpec(memory_space=pltpu.SMEM)
in_hbm = pl.BlockSpec(memory_space=pltpu.HBM)


def from_behind(shard, axis, by):
    size = lax.axis_size(axis)
    return lax.ppermute(shard, axis, [(i, (i + by) % size) for i in range(size)])


def local(array):
    return pltpu.with_memory_space_constraint(array, pltpu.VMEM)


def in_main(array):
    return pltpu.with_memory_space_constraint(array, pltpu.HBM)


def scalars(array):
    return pltpu.with_memory_space_constraint(array, pltpu.SMEM)


def run_copies(pairs, sems):
    copies = [
        pltpu.make_async_copy(source, target, sems.at[i]) for i, (source, target) in enumerate(pairs)
    ]
    for copy in copies:
        copy.start()
    for copy in copies:
        copy.wait()


def head_columns(index, width):
    return pl.ds(pl.multiple_of(index * width, width), width)


def wide(array):
    return jnp.concatenate([array, array], axis=1)


def halves(array):
    high = array.astype(bf16)
    low = (array - high.astype(f32)).astype(bf16)
    return high, low


def dot(left, right):
    return jnp.dot(left, right, preferred_element_type=f32)


def dot_nt(left, right):
    return lax.dot_general(left, right, (((1,), (1,)), ((), ())), preferred_element_type=f32)


def sigmoid(x):
    return 1.0 / (1.0 + jnp.exp(-x))


def pack_query(count, q_ref, *refs):
    outs, sems = refs[:-1], refs[-1]
    head = lax.axis_index("head")
    width = outs[0].shape[1]
    run_copies(
        [
            (q_ref.at[0, :, head_columns(lax.rem(head + s, count), width)], outs[s - 1])
            for s in range(1, count)
        ],
        sems,
    )


def pack_rest(count, q_ref, k_ref, v_ref, gu_ref, dn_ref, ids_ref, len_ref, *refs):
    own_q, own_k, own_v, packed, flags = refs[:5]
    sent_k, sent_v = refs[5 : 4 + count], refs[4 + count : 3 + 2 * count]
    ids, lens, sems = refs[-3:]
    head = lax.axis_index("head")
    here = lax.axis_index("ctx")
    width = own_q.shape[1]
    pairs = []
    for s in range(1, count):
        columns = head_columns(lax.rem(head + s, count), width)
        pairs.append((k_ref.at[0, :, columns], sent_k[s - 1]))
        pairs.append((v_ref.at[0, :, columns], sent_v[s - 1]))
    columns = head_columns(head, width)
    for whole_ref, own in ((q_ref, own_q), (k_ref, own_k), (v_ref, own_v)):
        pairs.append((whole_ref.at[0, :, columns], own))
    pairs.append((gu_ref.at[0, 0, 0], packed.at[0:width]))
    pairs.append((gu_ref.at[0, 0, 1], packed.at[width : 2 * width]))
    for group in range(dn_ref.shape[2] // width):
        rows = slice(group * width, (group + 1) * width)
        pairs.append((dn_ref.at[0, 0, rows], packed.at[2 * width : 3 * width, rows]))
    pairs.append((ids_ref, ids))
    pairs.append((len_ref, lens))
    run_copies(pairs, sems)
    size = ids.shape[1]
    before = lax.rem(here + size - 1, size)
    flags[0] = (ids[1, here] == ids[0, before]).astype(jnp.int32)
    flags[1] = lens[0, here]


def fast_forward(
    count, flags, packed, fresh_gu, fresh_dn, gain, rates, own_q, *refs
):
    got_q = refs[: count - 1]
    all_q, normed, weights, rate_row = refs[count - 1 :]
    rows, width = own_q.shape
    hidden = packed.shape[1]
    head = lax.axis_index("head")
    linked = flags[0] == 1
    length = flags[1]
    all_q[pl.ds(pl.multiple_of(head * rows, rows), rows), :] = own_q[...]
    for s in range(1, count):
        source = lax.rem(head + count - s, count)
        all_q[pl.ds(pl.multiple_of(source * rows, rows), rows), :] = got_q[s - 1][...]
    w_gate = jnp.where(linked, packed[0:width], fresh_gu[0, 0])
    w_up = jnp.where(linked, packed[width : 2 * width], fresh_gu[0, 1])
    down = [
        jnp.where(
            linked,
            packed[2 * width : 3 * width, g * width : (g + 1) * width],
            fresh_dn[0, g * width : (g + 1) * width],
        )
        for g in range(hidden // width)
    ]
    w_down = jnp.concatenate(down, axis=0)
    weights[0:width] = w_gate
    weights[width : 2 * width] = w_up
    for g in range(hidden // width):
        weights[2 * width : 3 * width, g * width : (g + 1) * width] = down[g]
    total = all_q.shape[0]
    token = lax.broadcasted_iota(jnp.int32, (1, total), 1)
    rate_row[...] = jnp.where(token < length, -rates[0], 0.0)
    gate2 = jnp.concatenate(halves(w_gate), axis=0)
    up2 = jnp.concatenate(halves(w_up), axis=0)
    down_high, down_low = halves(w_down)
    down2 = jnp.concatenate([down_high, down_low], axis=1)
    step = min(256, total)
    for start in range(0, total, step):
        block = all_q[start : start + step, :]
        block32 = block.astype(f32)
        unit = lax.rsqrt(jnp.mean(block32 * block32, axis=-1, keepdims=True) + epsilon)
        block2 = wide(block)
        gate = dot(block2, gate2) * unit
        up = dot(block2, up2) * unit
        high, low = halves(gate * sigmoid(gate) * up)
        both = dot(high, down2)
        fast = both[:, :width] + both[:, width:] + dot(low, down_high)
        scale = lax.rsqrt(jnp.mean(fast * fast, axis=-1, keepdims=True) + epsilon)
        row = start + lax.broadcasted_iota(jnp.int32, (step, 1), 0)
        scale = jnp.where(row < length, scale, 0.0)
        normed[start : start + step, :] = fast * scale * gain[...]


def attention_weights(count, tile, flags, all_q, tail_k, own_k, *refs):
    got_k = refs[: count - 1]
    keys, weights = refs[count - 1 :]
    rows, width = own_k.shape
    window = tail_k.shape[0]
    total = all_q.shape[0]
    head = lax.axis_index("head")
    linked = flags[0] == 1
    length = flags[1]
    keys[0:window, :] = tail_k[...]
    keys[pl.ds(pl.multiple_of(window + head * rows, 128), rows), :] = own_k[...]
    for s in range(1, count):
        source = lax.rem(head + count - s, count)
        keys[pl.ds(pl.multiple_of(window + source * rows, 128), rows), :] = got_k[s - 1][...]
    place = lax.broadcasted_iota(jnp.int32, (1, window + total), 1) - window
    open_key = (place < length) & ((place >= 0) | linked)
    bias = jnp.where(open_key, 0.0, masked)
    row = lax.broadcasted_iota(jnp.int32, (tile, tile), 0)
    column = lax.broadcasted_iota(jnp.int32, (tile, tile), 1)
    later = column > row
    same = column == row
    factor = math.log2(math.e) / math.sqrt(width)
    for index in range(total // tile):
        start = index * tile
        scores = dot_nt(all_q[start : start + tile, :], keys[start : start + tile + window, :])
        scores = scores * factor
        here = bias[:, start : start + tile + window]
        first = jnp.where(later, scores[:, :tile] + here[:, :tile], masked)
        middle = scores[:, tile:window] + here[:, tile:window]
        last = scores[:, window:]
        last = jnp.where(same, last, last + here[:, window:])
        last = jnp.where(later, masked, last)
        parts = [(0, first), (window, last)]
        if tile < window:
            parts.append((tile, middle))
        largest = functools.reduce(
            jnp.maximum, [jnp.max(part, axis=-1, keepdims=True) for _, part in parts]
        )
        parts = [(offset, jnp.exp2(part - largest)) for offset, part in parts]
        total_weight = sum(jnp.sum(part, axis=-1, keepdims=True) for _, part in parts)
        place_row = start + lax.broadcasted_iota(jnp.int32, (tile, 1), 0)
        scale = jnp.where(place_row < length, 1.0 / total_weight, 0.0)
        for offset, part in parts:
            weights[index, :, offset : offset + part.shape[1]] = (part * scale).astype(bf16)


def mixed_rows(tile, device, rows, weights, values, normed, out):
    window = weights.shape[2] - tile
    for t in range(rows // tile):
        start = pl.multiple_of(device * rows + t * tile, tile)
        index = device * (rows // tile) + t
        attended = dot(weights[index], values[pl.ds(start, tile + window), :])
        out[t * tile : (t + 1) * tile, :] = (attended + normed[pl.ds(start, tile), :]).astype(bf16)


def mix_sent(count, tile, weights, normed, tail_v, own_v, *refs):
    got_v = refs[: count - 1]
    values = refs[count - 1]
    outs = refs[count:]
    rows, width = own_v.shape
    window = tail_v.shape[0]
    head = lax.axis_index("head")
    values[0:window, :] = tail_v[...]
    values[pl.ds(pl.multiple_of(window + head * rows, 128), rows), :] = own_v[...]
    for s in range(1, count):
        source = lax.rem(head + count - s, count)
        values[pl.ds(pl.multiple_of(window + source * rows, 128), rows), :] = got_v[s - 1][...]
    for s in range(1, count):
        mixed_rows(
            tile, lax.rem(head + s, count), rows, weights, values, normed, outs[s - 1]
        )


def renormed(old_weight, gradient, axis):
    new_weight = old_weight - gradient
    old_square = jnp.mean(old_weight * old_weight, axis=axis, keepdims=True) + epsilon
    new_square = jnp.mean(new_weight * new_weight, axis=axis, keepdims=True) + epsilon
    return new_weight * (jnp.sqrt(old_square) / jnp.sqrt(new_square))


def update(
    tile, rows, weights, normed, values, keys, fast_weights, rate_row, mixed, new_gu, new_dn, own,
    gu, dn, sems,
):
    width = keys.shape[1]
    window = weights.shape[2] - tile
    hidden = fast_weights.shape[1]
    total = keys.shape[0] - window
    head = lax.axis_index("head")
    mixed_rows(tile, head, rows, weights, values, normed, own)
    out_copy = pltpu.make_async_copy(own, mixed.at[0, :, head_columns(head, width)], sems.at[0])
    out_copy.start()
    w_gate = fast_weights[0:width].T
    w_up = fast_weights[width : 2 * width].T
    w_down = jnp.concatenate(
        [
            fast_weights[2 * width : 3 * width, g * width : (g + 1) * width]
            for g in range(hidden // width)
        ],
        axis=0,
    )
    gate_up = jnp.concatenate(
        [
            jnp.concatenate(halves(w_gate), axis=1),
            jnp.concatenate(halves(w_up), axis=1),
        ],
        axis=0,
    )
    down = jnp.concatenate(halves(w_down), axis=1)
    ones = jnp.ones((8, 2 * width), bf16)
    grad_pair = jnp.zeros((2 * hidden, width), f32)
    grad_down = jnp.zeros((hidden, width), f32)
    step = min(256, total)
    for start in range(0, total, step):
        block_k = keys[window + start : window + start + step, :]
        block_v = values[window + start : window + start + step, :]
        block32 = block_k.astype(f32)
        square = jnp.concatenate(halves(block32 * block32), axis=1)
        unit = lax.rsqrt(dot_nt(ones, square)[:1] * (1.0 / width) + epsilon)
        both = dot_nt(gate_up, wide(block_k))
        gate = both[:hidden] * unit
        up = both[hidden:] * unit
        rate = rate_row[:, start : start + step]
        hidden_grad = dot_nt(down, wide(block_v)) * (rate * unit)
        share = sigmoid(gate)
        act = gate * share
        high_down, low_down = halves(act * up * rate)
        high_up, low_up = halves(hidden_grad * act)
        high_gate, low_gate = halves(hidden_grad * up * (share * (1.0 + gate * (1.0 - share))))
        stacked = jnp.concatenate([high_gate, high_up, low_gate, low_up], axis=0)
        pair = dot(stacked, block_k)
        grad_pair = grad_pair + (pair[: 2 * hidden] + pair[2 * hidden :])
        lower = dot(jnp.concatenate([high_down, low_down], axis=0), block_v)
        grad_down = grad_down + (lower[:hidden] + lower[hidden:])
    gu[0] = renormed(w_gate, grad_pair[:hidden], 1).T
    gu[1] = renormed(w_up, grad_pair[hidden:], 1).T
    dn[...] = renormed(w_down, grad_down, 0)
    first = pltpu.make_async_copy(gu, new_gu.at[0, 0], sems.at[1])
    second = pltpu.make_async_copy(dn, new_dn.at[0, 0], sems.at[2])
    first.start()
    second.start()
    out_copy.wait()
    first.wait()
    second.wait()


def place_received(count, *refs):
    got = refs[1:count]
    mixed, sems = refs[count:]
    width = got[0].shape[1]
    head = lax.axis_index("head")
    run_copies(
        [
            (got[s - 1], mixed.at[0, :, head_columns(lax.rem(head + count - s, count), width)])
            for s in range(1, count)
        ],
        sems,
    )


def params():
    return pltpu.CompilerParams(vmem_limit_bytes=24 * 1024 * 1024)


def on_device(
    queries,
    keys,
    values,
    rates,
    tail_keys,
    tail_values,
    state_in_gu,
    state_in_down,
    fresh_gu,
    fresh_down,
    out_gain,
    seq_ids,
    live_lengths,
):
    count = lax.axis_size("head")
    rows = queries.shape[1]
    width = queries.shape[2] // count
    window = tail_keys.shape[0]
    hidden = state_in_down.shape[2]
    total = rows * count
    tile = min(256, rows)
    piece = VMEM((rows, width), bf16)
    shifts = range(1, count)
    dma = pltpu.SemaphoreType.DMA

    sent_q = pl.pallas_call(
        functools.partial(pack_query, count),
        out_shape=[piece] * (count - 1),
        in_specs=[in_hbm],
        out_specs=[in_vmem] * (count - 1),
        scratch_shapes=[dma((count - 1,))],
        compiler_params=params(),
        name="pack_query",
    )(in_main(queries))
    got_q = [from_behind(sent_q[s - 1], "head", s) for s in shifts]
    packed_shape = VMEM((3 * width, hidden), f32)
    outs = pl.pallas_call(
        functools.partial(pack_rest, count),
        out_shape=[piece] * 3
        + [packed_shape, pltpu.SMEM((2,), jnp.int32)]
        + [piece] * (2 * count - 2),
        in_specs=[in_hbm] * 7,
        out_specs=[in_vmem] * 4 + [in_smem] + [in_vmem] * (2 * count - 2),
        scratch_shapes=[
            pltpu.SMEM(seq_ids.shape[::-1], jnp.int32),
            pltpu.SMEM(live_lengths.shape[::-1], jnp.int32),
            dma((2 * count + 5 + hidden // width,)),
        ],
        compiler_params=params(),
        name="pack_rest",
    )(
        *map(
            in_main,
            (queries, keys, values, state_in_gu, state_in_down, seq_ids.T, live_lengths.T),
        )
    )
    own_q, own_k, own_v, packed, flags = outs[:5]
    sent_k, sent_v = outs[5 : 4 + count], outs[4 + count :]
    moved = from_behind(packed, "ctx", 1)
    got_k = [from_behind(sent_k[s - 1], "head", s) for s in shifts]
    prior_keys = from_behind(tail_keys, "ctx", 1)
    got_v = [from_behind(sent_v[s - 1], "head", s) for s in shifts]
    prior_values = from_behind(tail_values, "ctx", 1)

    all_q, normed, fast_weights, rate_row = pl.pallas_call(
        functools.partial(fast_forward, count),
        out_shape=[
            VMEM((total, width), bf16),
            VMEM((total, width), f32),
            packed_shape,
            VMEM((1, total), f32),
        ],
        in_specs=[in_smem] + [in_vmem] * (5 + count),
        out_specs=[in_vmem] * 4,
        compiler_params=params(),
        name="fast_forward",
    )(
        scalars(flags),
        *map(local, (moved, fresh_gu, fresh_down, out_gain[None], rates, own_q, *got_q)),
    )
    joined = VMEM((window + total, width), bf16)
    all_keys, weights = pl.pallas_call(
        functools.partial(attention_weights, count, tile),
        out_shape=[joined, VMEM((total // tile, tile, tile + window), bf16)],
        in_specs=[in_smem] + [in_vmem] * (2 + count),
        out_specs=[in_vmem] * 2,
        compiler_params=params(),
        name="attention_weights",
    )(scalars(flags), *map(local, (all_q, prior_keys, own_k, *got_k)))
    all_values, *mixed_out = pl.pallas_call(
        functools.partial(mix_sent, count, tile),
        out_shape=[joined] + [piece] * (count - 1),
        in_specs=[in_vmem] * (3 + count),
        out_specs=[in_vmem] * count,
        compiler_params=params(),
        name="mix_sent",
    )(*map(local, (weights, normed, prior_values, own_v, *got_v)))
    mixed_in = [from_behind(mixed_out[s - 1], "head", s) for s in shifts]
    mixed, new_gu, new_down = pl.pallas_call(
        functools.partial(update, tile, rows),
        out_shape=[
            jax.ShapeDtypeStruct(queries.shape, bf16),
            jax.ShapeDtypeStruct(state_in_gu.shape, f32),
            jax.ShapeDtypeStruct(state_in_down.shape, f32),
        ],
        in_specs=[in_vmem] * 6,
        out_specs=[in_hbm] * 3,
        scratch_shapes=[
            VMEM((rows, width), bf16),
            VMEM(state_in_gu.shape[2:], f32),
            VMEM(state_in_down.shape[2:], f32),
            dma((3,)),
        ],
        compiler_params=params(),
        name="update",
    )(*map(local, (weights, normed, all_values, all_keys, fast_weights, rate_row)))
    mixed = pl.pallas_call(
        functools.partial(place_received, count),
        out_shape=jax.ShapeDtypeStruct(queries.shape, bf16),
        in_specs=[in_hbm] + [in_vmem] * (count - 1),
        out_specs=in_hbm,
        scratch_shapes=[dma((count - 1,))],
        input_output_aliases={0: 0},
        compiler_params=params(),
        name="place_received",
    )(in_main(mixed), *map(local, mixed_in))
    return (mixed, new_gu, new_down)


def solution(mesh):
    placed = (
        P(None, ("ctx", "head"), None),
        P(None, ("ctx", "head"), None),
        P(None, ("ctx", "head"), None),
        P(None, "head", "ctx"),
        P("ctx", "head"),
        P("ctx", "head"),
        P("ctx", "head", None, None, None),
        P("ctx", "head", None, None),
        P("head", None, None, None),
        P("head", None, None),
        P("head"),
        P(),
        P(),
    )
    return jax.shard_map(
        on_device,
        mesh=mesh,
        in_specs=placed,
        out_specs=(
            P(None, ("ctx", "head"), None),
            P("ctx", "head", None, None, None),
            P("ctx", "head", None, None),
        ),
        check_vma=False,
    )
```

```python
import functools
import math

import jax
import jax.numpy as jnp
from jax import lax
from jax.experimental import pallas as pl
from jax.experimental.pallas import tpu as pltpu
from jax.sharding import PartitionSpec as P

epsilon = 1e-06
masked = -1e30
f32 = jnp.float32
bf16 = jnp.bfloat16

VMEM = pltpu.VMEM
in_vmem = pl.BlockSpec(memory_space=pltpu.VMEM)
in_smem = pl.BlockSpec(memory_space=pltpu.SMEM)
in_hbm = pl.BlockSpec(memory_space=pltpu.HBM)


def from_behind(shard, axis, by):
    size = lax.axis_size(axis)
    return lax.ppermute(shard, axis, [(i, (i + by) % size) for i in range(size)])


def local(array):
    return pltpu.with_memory_space_constraint(array, pltpu.VMEM)


def in_main(array):
    return pltpu.with_memory_space_constraint(array, pltpu.HBM)


def scalars(array):
    return pltpu.with_memory_space_constraint(array, pltpu.SMEM)


def run_copies(pairs, sems):
    copies = [
        pltpu.make_async_copy(source, target, sems.at[i]) for i, (source, target) in enumerate(pairs)
    ]
    for copy in copies:
        copy.start()
    for copy in copies:
        copy.wait()


def head_columns(index, width):
    return pl.ds(pl.multiple_of(index * width, width), width)


def wide(array):
    return jnp.concatenate([array, array], axis=1)


def halves(array):
    high = array.astype(bf16)
    low = (array - high.astype(f32)).astype(bf16)
    return high, low


def dot(left, right):
    return jnp.dot(left, right, preferred_element_type=f32)


def dot_nt(left, right):
    return lax.dot_general(left, right, (((1,), (1,)), ((), ())), preferred_element_type=f32)


def sigmoid(x):
    return 0.5 * jnp.tanh(0.5 * x) + 0.5


def row_block(index, rows):
    return pl.ds(pl.multiple_of(index * rows, rows), rows)


def fast_rows(high, low, first_row, length, down2, gain):
    count = high.shape[0]
    width = down2.shape[1] // 2
    both = dot(high, down2[...])
    fast = both[:, :width] + both[:, width:] + dot(low, down2[:, :width])
    scale = lax.rsqrt(jnp.mean(fast * fast, axis=-1, keepdims=True) + epsilon)
    row = first_row + lax.broadcasted_iota(jnp.int32, (count, 1), 0)
    return fast * jnp.where(row < length, scale, 0.0) * gain[...]


def store_weights(queries, keys, first_row, length, linked, out):
    tile, width = queries.shape
    window = keys.shape[0] - tile
    place = first_row - window + lax.broadcasted_iota(jnp.int32, (1, tile + window), 1)
    bias = jnp.where((place < length) & ((place >= 0) | linked), 0.0, masked)
    row = lax.broadcasted_iota(jnp.int32, (tile, tile), 0)
    column = lax.broadcasted_iota(jnp.int32, (tile, tile), 1)
    later = column > row
    factor = math.log2(math.e) / math.sqrt(width)
    scores = dot_nt(queries, keys) * factor
    first = jnp.where(later, scores[:, :tile] + bias[:, :tile], masked)
    last = scores[:, window:]
    last = jnp.where(column == row, last, last + bias[:, window:])
    last = jnp.where(later, masked, last)
    parts = [(0, first), (window, last)]
    if tile < window:
        parts.append((tile, scores[:, tile:window] + bias[:, tile:window]))
    largest = functools.reduce(
        jnp.maximum, [jnp.max(part, axis=-1, keepdims=True) for _, part in parts]
    )
    parts = [(offset, jnp.exp2(part - largest)) for offset, part in parts]
    total = sum(jnp.sum(part, axis=-1, keepdims=True) for _, part in parts)
    token = first_row + lax.broadcasted_iota(jnp.int32, (tile, 1), 0)
    scale = jnp.where(token < length, 1.0 / total, 0.0)
    for offset, part in parts:
        out[:, offset : offset + part.shape[1]] = (part * scale).astype(bf16)


def join(count, window, own, got, joined):
    rows = own.shape[0]
    head = lax.axis_index("head")
    joined[pl.ds(pl.multiple_of(window + head * rows, rows), rows), :] = own[...]
    for s in range(1, count):
        source = lax.rem(head + count - s, count)
        joined[pl.ds(pl.multiple_of(window + source * rows, rows), rows), :] = got[s - 1][...]


def pack(count, k_ref, v_ref, dn_ref, tail_k, tail_v, *refs):
    down_keys, last_v = refs[:2]
    sent_k, sent_v = refs[2 : 1 + count], refs[1 + count : 2 * count]
    down, sems = refs[-2:]
    head = lax.axis_index("head")
    hidden, width = down.shape
    pairs = [(dn_ref.at[0, 0], down)]
    for s in range(1, count):
        columns = head_columns(lax.rem(head + s, count), width)
        pairs.append((k_ref.at[0, :, columns], sent_k[s - 1]))
        pairs.append((v_ref.at[0, :, columns], sent_v[s - 1]))
    pairs += [(tail_k, down_keys.at[2 * hidden :]), (tail_v, last_v)]
    run_copies(pairs, sems)
    high, low = halves(down[...])
    down_keys[0:hidden] = high
    down_keys[hidden : 2 * hidden] = low


def load(
    count, k_ref, v_ref, fresh_gu, fresh_dn, gain, rates, ids_ref, len_ref, _, own_k, own_v, fresh,
    gain_row, rate_row, flags, ids, lens, sems
):
    head = lax.axis_index("head")
    here = lax.axis_index("ctx")
    width = own_k.shape[1]
    columns = head_columns(head, width)
    pairs = [
        (k_ref.at[0, :, columns], own_k),
        (v_ref.at[0, :, columns], own_v),
        (fresh_gu.at[0, 0], fresh.at[0:width]),
        (fresh_gu.at[0, 1], fresh.at[width : 2 * width]),
    ]
    for group in range(fresh_dn.shape[1] // width):
        part = slice(group * width, (group + 1) * width)
        pairs.append((fresh_dn.at[0, part], fresh.at[2 * width : 3 * width, part]))
    pairs += [(gain, gain_row), (rates.at[0], rate_row), (ids_ref, ids), (len_ref, lens)]
    run_copies(pairs, sems)
    size = ids.shape[1]
    before = lax.rem(here + size - 1, size)
    flags[0] = (ids[1, here] == ids[0, before]).astype(jnp.int32)
    flags[1] = lens[0, here]


def join_queries(*refs):
    joined = refs[-1]
    rows = refs[0].shape[0]
    for index, part in enumerate(refs[:-1]):
        joined[index * rows : (index + 1) * rows, :] = part[...]


def query_hidden(queries, gate2, up2, highs, lows):
    total, width = queries.shape
    step = min(256, total)
    for start in range(0, total, step):
        block = queries[start : start + step, :]
        block32 = block.astype(f32)
        unit = lax.rsqrt(jnp.mean(block32 * block32, axis=-1, keepdims=True) + epsilon)
        doubled = wide(block)
        gate = dot(doubled, gate2[...]) * unit
        up = dot(doubled, up2[...]) * unit
        high, low = halves(gate * sigmoid(gate) * up)
        highs[start : start + step, :] = high
        lows[start : start + step, :] = low


def choose_gate_up(flags, _, got_gu, fresh, rates, gate2, up2, turned2, turned, rate_row):
    hidden = fresh.shape[1]
    width = got_gu.shape[0] // 2
    linked = flags[0] == 1
    length = flags[1]
    for index, split in enumerate((gate2, up2)):
        rows = slice(index * width, (index + 1) * width)
        weight = jnp.where(linked, got_gu[rows], fresh[rows])
        split[...] = jnp.concatenate(halves(weight), axis=0)
        part = slice(index * hidden, (index + 1) * hidden)
        weight = weight.T
        turned[part] = weight
        turned2[part] = jnp.concatenate(halves(weight), axis=1)
    token = lax.broadcasted_iota(jnp.int32, rates.shape, 1)
    rate_row[...] = jnp.where(token < length, -rates[...], 0.0)


def key_hidden(
    count, window, _, turned2, rate_row, own_k, *refs
):
    got_k, (keys, gate_part, up_part, down_steps) = refs[: count - 1], refs[count - 1 :]
    rows, width = own_k.shape
    hidden = turned2.shape[0] // 2
    total = count * rows
    join(count, window, own_k, got_k, keys)
    ones = jnp.ones((8, 2 * width), bf16)
    step = min(256, total)
    for start in range(0, total, step):
        block = keys[window + start : window + start + step, :]
        block32 = block.astype(f32)
        square = jnp.concatenate(halves(block32 * block32), axis=1)
        unit = lax.rsqrt(dot_nt(ones, square)[:1] * (1.0 / width) + epsilon)
        rate = rate_row[:, start : start + step]
        scale = rate * unit
        both = dot_nt(turned2[...], wide(block))
        gate = both[:hidden] * unit
        up = both[hidden:] * unit
        share = sigmoid(gate)
        act = gate * share
        gate_part[:, start : start + step] = up * (share + act * (1.0 - share)) * scale
        up_part[:, start : start + step] = act * scale
        down_steps[:, start : start + step] = (act * up * rate).astype(bf16)


def choose_down(flags, down_keys, fresh, keys, down2, down, joined):
    hidden, width = down.shape
    window = down_keys.shape[0] - 2 * hidden
    linked = flags[0] == 1
    fresh_down = jnp.concatenate(
        [fresh[2 * width :, g * width : (g + 1) * width] for g in range(hidden // width)], axis=0
    )
    got_down = down_keys[0:hidden].astype(f32) + down_keys[hidden : 2 * hidden].astype(f32)
    w_down = jnp.where(linked, got_down, fresh_down)
    down[...] = w_down
    down2[...] = jnp.concatenate(halves(w_down), axis=1)
    joined[0:window] = down_keys[2 * hidden :]


def sent_rows(count, tile, flags, down2, gain, keys, queries, highs, lows, weights, normed):
    rows = queries.shape[0] // count
    window = keys.shape[0] - count * rows
    linked = flags[0] == 1
    length = flags[1]
    head = lax.axis_index("head")
    for s in range(1, count):
        device = lax.rem(head + s, count)
        for t in range(rows // tile):
            place = (s - 1) * rows + t * tile
            start = pl.multiple_of(device * rows + t * tile, tile)
            span = slice(place, place + tile)
            normed[span, :] = fast_rows(highs[span, :], lows[span, :], start, length, down2, gain)
            store_weights(
                queries[span, :],
                keys[pl.ds(start, tile + window), :],
                start,
                length,
                linked,
                weights.at[place // tile],
            )


def start_values(_, tail_v, own_v, values):
    window = tail_v.shape[0]
    values[0:window, :] = tail_v[...]
    join(1, window, own_v, [], values)


def mix_sent(count, weights, normed, _, *refs):
    got_v, values, outs = refs[: count - 1], refs[count - 1], refs[count:]
    rows = got_v[0].shape[0]
    tile, span = weights.shape[1:]
    head = lax.axis_index("head")
    for s in range(1, count):
        source = lax.rem(head + count - s, count)
        start = span - tile + source * rows
        values[pl.ds(pl.multiple_of(start, rows), rows), :] = got_v[s - 1][...]
    for s in range(1, count):
        device = lax.rem(head + s, count)
        for t in range(rows // tile):
            place = (s - 1) * rows + t * tile
            start = pl.multiple_of(device * rows + t * tile, tile)
            attended = dot(weights[place // tile], values[pl.ds(start, span), :])
            outs[s - 1][t * tile : (t + 1) * tile, :] = (
                attended + normed[place : place + tile, :]
            ).astype(bf16)


def renormed(old_weight, gradient, axis):
    new_weight = old_weight - gradient
    old_square = jnp.mean(old_weight * old_weight, axis=axis, keepdims=True) + epsilon
    new_square = jnp.mean(new_weight * new_weight, axis=axis, keepdims=True) + epsilon
    return new_weight * (jnp.sqrt(old_square) / jnp.sqrt(new_square))


def own_rows_and_update(
    tile,
    flags,
    down2,
    gain,
    queries,
    highs,
    lows,
    keys,
    values,
    turned,
    down,
    gate_part,
    up_part,
    down_steps,
    mixed,
    new_gu,
    new_dn,
    weights,
    own,
    steps,
    gu,
    dn,
    sems,
):
    rows, width = own.shape
    hidden = down.shape[0]
    window = weights.shape[1] - tile
    total = keys.shape[0] - window
    linked = flags[0] == 1
    length = flags[1]
    head = lax.axis_index("head")
    for t in range(rows // tile):
        start = pl.multiple_of(head * rows + t * tile, tile)
        place = total - rows + t * tile
        span = slice(place, place + tile)
        normed = fast_rows(highs[span, :], lows[span, :], start, length, down2, gain)
        store_weights(
            queries[span, :], keys[pl.ds(start, tile + window), :], start, length, linked, weights
        )
        attended = dot(weights[...], values[pl.ds(start, tile + window), :])
        own[t * tile : (t + 1) * tile, :] = (attended + normed).astype(bf16)
    out_copy = pltpu.make_async_copy(own, mixed.at[0, :, head_columns(head, width)], sems.at[0])
    out_copy.start()
    step = min(256, total)
    for start in range(0, total, step):
        block_v = values[window + start : window + start + step, :]
        hidden_grad = dot_nt(down2[...], wide(block_v))
        part = slice(start, start + step)
        steps[0:hidden, part] = (hidden_grad * gate_part[:, part]).astype(bf16)
        steps[hidden : 2 * hidden, part] = (hidden_grad * up_part[:, part]).astype(bf16)
    both = dot(steps[...], keys[window:, :])
    for index in range(2):
        part = slice(index * hidden, (index + 1) * hidden)
        gu[index] = renormed(turned[part], both[part], 1).T
    first = pltpu.make_async_copy(gu, new_gu.at[0, 0], sems.at[1])
    first.start()
    dn[...] = renormed(down[...], dot(down_steps[...], values[window:, :]), 0)
    second = pltpu.make_async_copy(dn, new_dn.at[0, 0], sems.at[2])
    second.start()
    out_copy.wait()
    first.wait()
    second.wait()


def place_received(count, *refs):
    got = refs[1:count]
    mixed, sems = refs[count:]
    width = got[0].shape[1]
    head = lax.axis_index("head")
    run_copies(
        [
            (got[s - 1], mixed.at[0, :, head_columns(lax.rem(head + count - s, count), width)])
            for s in range(1, count)
        ],
        sems,
    )


def params():
    return pltpu.CompilerParams(vmem_limit_bytes=24 * 1024 * 1024)


def call(body, name, outs, ins, scratch=(), cost=1, aliases={}):
    spec = {local: in_vmem, in_main: in_hbm, scalars: in_smem}
    return pl.pallas_call(
        body,
        out_shape=[shape for _, shape in outs],
        in_specs=[spec[where] for where, _ in ins],
        out_specs=[spec[where] for where, _ in outs],
        scratch_shapes=list(scratch),
        input_output_aliases=aliases,
        compiler_params=params(),
        cost_estimate=pl.CostEstimate(
            flops=int(cost * 1e6), bytes_accessed=1024, transcendentals=0
        ),
        name=name,
    )(*[where(array) for where, array in ins])


def on_device(
    queries,
    keys,
    values,
    rates,
    tail_keys,
    tail_values,
    state_in_gu,
    state_in_down,
    fresh_gu,
    fresh_down,
    out_gain,
    seq_ids,
    live_lengths,
):
    count = lax.axis_size("head")
    rows = queries.shape[1]
    width = queries.shape[2] // count
    window = tail_keys.shape[0]
    hidden = state_in_down.shape[2]
    total = rows * count
    sent = total - rows
    tile = min(256, rows)
    span = tile + window
    shifts = range(1, count)
    dma = pltpu.SemaphoreType.DMA

    def on_chip(shape, kind):
        return (local, VMEM(shape, kind))

    def in_hbm_out(shape, kind):
        return (in_main, jax.ShapeDtypeStruct(shape, kind))

    def all_local(*arrays):
        return [(local, array) for array in arrays]

    piece = on_chip((rows, width), bf16)

    def columns(array, shift):
        start = lax.rem(lax.axis_index("head") + shift, count) * width
        return lax.dynamic_slice_in_dim(array[0], start, width, 1)

    sent_q = [columns(queries, s) for s in shifts]
    got_q = [from_behind(sent_q[s - 1], "head", s) for s in shifts]
    own_q = columns(lax.optimization_barrier((queries, *sent_q))[0], 0)
    got_gu = from_behind(state_in_gu[0, 0].reshape(2 * width, hidden), "ctx", 1)
    down_keys, last_v, *packed = call(
        functools.partial(pack, count),
        "pack",
        [on_chip((2 * hidden + window, width), bf16), on_chip((window, width), bf16)]
        + [piece] * (2 * count - 2),
        [(in_main, array) for array in (keys, values, state_in_down, tail_keys, tail_values)],
        scratch=[VMEM((hidden, width), f32), dma((2 * count + 1,))],
    )
    sent_k, sent_v = packed[: count - 1], packed[count - 1 :]
    got_k = [from_behind(sent_k[s - 1], "head", s) for s in shifts]
    got_dk = from_behind(down_keys, "ctx", 1)
    prior_v = from_behind(last_v, "ctx", 1)
    got_v = [from_behind(sent_v[s - 1], "head", s) for s in shifts]

    own_k, own_v, fresh, gain, rate_row, flags = call(
        functools.partial(load, count),
        "load",
        [
            piece,
            piece,
            on_chip((3 * width, hidden), f32),
            on_chip((1, width), f32),
            on_chip((1, total), f32),
            (scalars, pltpu.SMEM((2,), jnp.int32)),
        ],
        [
            (in_main, array)
            for array in (
                keys,
                values,
                fresh_gu,
                fresh_down,
                out_gain[None],
                rates,
                seq_ids.T,
                live_lengths.T,
            )
        ]
        + all_local(got_q[0]),
        scratch=[
            pltpu.SMEM(seq_ids.shape[::-1], jnp.int32),
            pltpu.SMEM(live_lengths.shape[::-1], jnp.int32),
            dma((8 + hidden // width,)),
        ],
    )
    (all_q,) = call(
        join_queries,
        "join_queries",
        [on_chip((total, width), bf16)],
        all_local(*got_q[::-1], own_q),
        cost=90,
    )
    gate2, up2, turned2, turned, live_rates = call(
        choose_gate_up,
        "choose_gate_up",
        [
            on_chip((2 * width, hidden), bf16),
            on_chip((2 * width, hidden), bf16),
            on_chip((2 * hidden, 2 * width), bf16),
            on_chip((2 * hidden, width), f32),
            on_chip((1, total), f32),
        ],
        [(scalars, flags)] + all_local(all_q, got_gu, fresh, rate_row),
        cost=90,
    )
    highs, lows = call(
        query_hidden,
        "query_hidden",
        [on_chip((total, hidden), bf16)] * 2,
        all_local(all_q, gate2, up2),
    )
    all_keys_shape = on_chip((window + total, width), bf16)
    all_keys, gate_part, up_part, down_steps = call(
        functools.partial(key_hidden, count, window),
        "key_hidden",
        [
            all_keys_shape,
            on_chip((hidden, total), f32),
            on_chip((hidden, total), f32),
            on_chip((hidden, total), bf16),
        ],
        all_local(highs, turned2, live_rates, own_k, *got_k),
        cost=1300,
    )
    down2, down, all_keys = call(
        choose_down,
        "choose_down",
        [on_chip((hidden, 2 * width), bf16), on_chip((hidden, width), f32), all_keys_shape],
        [(scalars, flags)] + all_local(got_dk, fresh, all_keys),
        aliases={3: 2},
    )
    weights, normed = call(
        functools.partial(sent_rows, count, tile),
        "sent_rows",
        [on_chip((sent // tile, tile, span), bf16), on_chip((sent, width), f32)],
        [(scalars, flags)] + all_local(down2, gain, all_keys, all_q, highs, lows),
        cost=50,
    )
    (all_values,) = call(
        start_values,
        "start_values",
        [on_chip((window + total, width), bf16)],
        all_local(normed, prior_v, own_v),
        cost=50,
    )
    all_values, *mixed_out = call(
        functools.partial(mix_sent, count),
        "mix_sent",
        [on_chip((window + total, width), bf16)] + [piece] * (count - 1),
        all_local(weights, normed, all_values, *got_v),
        aliases={2: 0},
    )
    mixed_in = [from_behind(mixed_out[s - 1], "head", s) for s in shifts]
    mixed, new_gu, new_down = call(
        functools.partial(own_rows_and_update, tile),
        "own_rows_and_update",
        [
            in_hbm_out(queries.shape, bf16),
            in_hbm_out(state_in_gu.shape, f32),
            in_hbm_out(state_in_down.shape, f32),
        ],
        [(scalars, flags)]
        + all_local(
            down2,
            gain,
            all_q,
            highs,
            lows,
            all_keys,
            all_values,
            turned,
            down,
            gate_part,
            up_part,
            down_steps,
        ),
        scratch=[
            VMEM((tile, span), bf16),
            VMEM((rows, width), bf16),
            VMEM((2 * hidden, total), bf16),
            VMEM(state_in_gu.shape[2:], f32),
            VMEM(state_in_down.shape[2:], f32),
            dma((3,)),
        ],
    )
    (mixed,) = call(
        functools.partial(place_received, count),
        "place_received",
        [in_hbm_out(queries.shape, bf16)],
        [(in_main, mixed)] + all_local(*mixed_in),
        scratch=[dma((count - 1,))],
        aliases={0: 0},
    )
    return (mixed, new_gu, new_down)


def solution(mesh):
    placed = (
        P(None, ("ctx", "head"), None),
        P(None, ("ctx", "head"), None),
        P(None, ("ctx", "head"), None),
        P(None, "head", "ctx"),
        P("ctx", "head"),
        P("ctx", "head"),
        P("ctx", "head", None, None, None),
        P("ctx", "head", None, None),
        P("head", None, None, None),
        P("head", None, None),
        P("head"),
        P(),
        P(),
    )
    return jax.shard_map(
        on_device,
        mesh=mesh,
        in_specs=placed,
        out_specs=(
            P(None, ("ctx", "head"), None),
            P("ctx", "head", None, None, None),
            P("ctx", "head", None, None),
        ),
        check_vma=False,
    )
```

```python
import functools
import math

import jax
import jax.numpy as jnp
from jax import lax
from jax.experimental import pallas as pl
from jax.experimental.pallas import tpu as pltpu
from jax.sharding import PartitionSpec as P

epsilon = 1e-06
masked = -1e30
f32 = jnp.float32
bf16 = jnp.bfloat16

VMEM = pltpu.VMEM
in_vmem = pl.BlockSpec(memory_space=pltpu.VMEM)
in_smem = pl.BlockSpec(memory_space=pltpu.SMEM)
in_hbm = pl.BlockSpec(memory_space=pltpu.HBM)


def from_behind(shard, axis, by):
    size = lax.axis_size(axis)
    return lax.ppermute(shard, axis, [(i, (i + by) % size) for i in range(size)])


def local(array):
    return pltpu.with_memory_space_constraint(array, pltpu.VMEM)


def in_main(array):
    return pltpu.with_memory_space_constraint(array, pltpu.HBM)


def scalars(array):
    return pltpu.with_memory_space_constraint(array, pltpu.SMEM)


def run_copies(pairs, sems):
    copies = [
        pltpu.make_async_copy(source, target, sems.at[i]) for i, (source, target) in enumerate(pairs)
    ]
    for copy in copies:
        copy.start()
    for copy in copies:
        copy.wait()


def head_columns(index, width):
    return pl.ds(pl.multiple_of(index * width, width), width)


def wide(array):
    return jnp.concatenate([array, array], axis=1)


def halves(array):
    high = array.astype(bf16)
    low = (array - high.astype(f32)).astype(bf16)
    return high, low


def dot(left, right):
    return jnp.dot(left, right, preferred_element_type=f32)


def dot_nt(left, right):
    return lax.dot_general(left, right, (((1,), (1,)), ((), ())), preferred_element_type=f32)


def sigmoid(x):
    return 0.5 * jnp.tanh(0.5 * x) + 0.5


def row_block(index, rows):
    return pl.ds(pl.multiple_of(index * rows, rows), rows)


def fast_rows(high, low, first_row, length, down2, gain):
    count = high.shape[0]
    width = down2.shape[1] // 2
    both = dot(high, down2[...])
    fast = both[:, :width] + both[:, width:] + dot(low, down2[:, :width])
    scale = lax.rsqrt(jnp.mean(fast * fast, axis=-1, keepdims=True) + epsilon)
    row = first_row + lax.broadcasted_iota(jnp.int32, (count, 1), 0)
    return fast * jnp.where(row < length, scale, 0.0) * gain[...]


def store_weights(queries, keys, first_row, length, linked, out):
    tile, width = queries.shape
    window = keys.shape[0] - tile
    place = first_row - window + lax.broadcasted_iota(jnp.int32, (1, tile + window), 1)
    bias = jnp.where((place < length) & ((place >= 0) | linked), 0.0, masked)
    row = lax.broadcasted_iota(jnp.int32, (tile, tile), 0)
    column = lax.broadcasted_iota(jnp.int32, (tile, tile), 1)
    later = column > row
    factor = math.log2(math.e) / math.sqrt(width)
    scores = dot_nt(queries, keys) * factor
    first = jnp.where(later, scores[:, :tile] + bias[:, :tile], masked)
    last = scores[:, window:]
    last = jnp.where(column == row, last, last + bias[:, window:])
    last = jnp.where(later, masked, last)
    parts = [(0, first), (window, last)]
    if tile < window:
        parts.append((tile, scores[:, tile:window] + bias[:, tile:window]))
    largest = functools.reduce(
        jnp.maximum, [jnp.max(part, axis=-1, keepdims=True) for _, part in parts]
    )
    parts = [(offset, jnp.exp2(part - largest)) for offset, part in parts]
    total = sum(jnp.sum(part, axis=-1, keepdims=True) for _, part in parts)
    token = first_row + lax.broadcasted_iota(jnp.int32, (tile, 1), 0)
    scale = jnp.where(token < length, 1.0 / total, 0.0)
    for offset, part in parts:
        out[:, offset : offset + part.shape[1]] = (part * scale).astype(bf16)


def join(count, window, own, got, joined):
    rows = own.shape[0]
    head = lax.axis_index("head")
    joined[pl.ds(pl.multiple_of(window + head * rows, rows), rows), :] = own[...]
    for s in range(1, count):
        source = lax.rem(head + count - s, count)
        joined[pl.ds(pl.multiple_of(window + source * rows, rows), rows), :] = got[s - 1][...]


def pack(count, q_ref, k_ref, v_ref, dn_ref, tail_k, tail_v, *refs):
    down_keys, last_v = refs[:2]
    sent_qk, sent_v = refs[2 : 1 + count], refs[1 + count : 2 * count]
    down, sems = refs[-2:]
    head = lax.axis_index("head")
    hidden, width = down.shape
    rows = sent_v[0].shape[0]
    pairs = [(dn_ref.at[0, 0], down)]
    for s in range(1, count):
        columns = head_columns(lax.rem(head + s, count), width)
        pairs.append((q_ref.at[0, :, columns], sent_qk[s - 1].at[0:rows]))
        pairs.append((k_ref.at[0, :, columns], sent_qk[s - 1].at[rows : 2 * rows]))
        pairs.append((v_ref.at[0, :, columns], sent_v[s - 1]))
    pairs += [(tail_k, down_keys.at[2 * hidden :]), (tail_v, last_v)]
    run_copies(pairs, sems)
    high, low = halves(down[...])
    down_keys[0:hidden] = high
    down_keys[hidden : 2 * hidden] = low


def load(
    count, q_ref, k_ref, v_ref, fresh_gu, fresh_dn, gain, rates, ids_ref, len_ref, _, own_q, own_k,
    own_v, fresh,
    gain_row, rate_row, flags, ids, lens, sems
):
    head = lax.axis_index("head")
    here = lax.axis_index("ctx")
    width = own_k.shape[1]
    columns = head_columns(head, width)
    pairs = [
        (q_ref.at[0, :, columns], own_q),
        (k_ref.at[0, :, columns], own_k),
        (v_ref.at[0, :, columns], own_v),
        (fresh_gu.at[0, 0], fresh.at[0:width]),
        (fresh_gu.at[0, 1], fresh.at[width : 2 * width]),
    ]
    for group in range(fresh_dn.shape[1] // width):
        part = slice(group * width, (group + 1) * width)
        pairs.append((fresh_dn.at[0, part], fresh.at[2 * width : 3 * width, part]))
    pairs += [(gain, gain_row), (rates.at[0], rate_row), (ids_ref, ids), (len_ref, lens)]
    run_copies(pairs, sems)
    size = ids.shape[1]
    before = lax.rem(here + size - 1, size)
    flags[0] = (ids[1, here] == ids[0, before]).astype(jnp.int32)
    flags[1] = lens[0, here]


def hidden_rows(queries, gate2, up2):
    queries32 = queries.astype(f32)
    unit = lax.rsqrt(jnp.mean(queries32 * queries32, axis=-1, keepdims=True) + epsilon)
    doubled = wide(queries)
    gate = dot(doubled, gate2[...]) * unit
    up = dot(doubled, up2[...]) * unit
    return halves(gate * sigmoid(gate) * up)


def sent_hidden(count, tile, window, gate2, up2, own_k, *refs):
    got_qk, (queries, highs, lows, keys) = refs[: count - 1], refs[count - 1 :]
    rows, width = own_k.shape
    for s in range(1, count):
        source = got_qk[count - s - 1]
        for t in range(rows // tile):
            span = slice((s - 1) * rows + t * tile, (s - 1) * rows + (t + 1) * tile)
            block = source[t * tile : (t + 1) * tile, :]
            queries[span, :] = block
            high, low = hidden_rows(block, gate2, up2)
            highs[span, :] = high
            lows[span, :] = low
    join(count, window, own_k, [got.at[rows : 2 * rows] for got in got_qk], keys)


def choose_gate_up(flags, got_gu, fresh, rates, gate2, up2, turned2, turned, rate_row):
    hidden = fresh.shape[1]
    width = got_gu.shape[0] // 2
    linked = flags[0] == 1
    length = flags[1]
    for index, split in enumerate((gate2, up2)):
        rows = slice(index * width, (index + 1) * width)
        weight = jnp.where(linked, got_gu[rows], fresh[rows])
        split[...] = jnp.concatenate(halves(weight), axis=0)
        part = slice(index * hidden, (index + 1) * hidden)
        weight = weight.T
        turned[part] = weight
        turned2[part] = jnp.concatenate(halves(weight), axis=1)
    token = lax.broadcasted_iota(jnp.int32, rates.shape, 1)
    rate_row[...] = jnp.where(token < length, -rates[...], 0.0)


def choose_down(flags, down_keys, fresh, keys, down2, down, joined):
    hidden, width = down.shape
    window = down_keys.shape[0] - 2 * hidden
    linked = flags[0] == 1
    fresh_down = jnp.concatenate(
        [fresh[2 * width :, g * width : (g + 1) * width] for g in range(hidden // width)], axis=0
    )
    got_down = down_keys[0:hidden].astype(f32) + down_keys[hidden : 2 * hidden].astype(f32)
    w_down = jnp.where(linked, got_down, fresh_down)
    down[...] = w_down
    down2[...] = jnp.concatenate(halves(w_down), axis=1)
    joined[0:window] = down_keys[2 * hidden :]


def sent_rows(count, tile, flags, down2, gain, keys, queries, highs, lows, weights, normed):
    rows = queries.shape[0] // (count - 1)
    window = keys.shape[0] - count * rows
    linked = flags[0] == 1
    length = flags[1]
    head = lax.axis_index("head")
    for s in range(1, count):
        device = lax.rem(head + s, count)
        for t in range(rows // tile):
            place = (s - 1) * rows + t * tile
            start = pl.multiple_of(device * rows + t * tile, tile)
            span = slice(place, place + tile)
            normed[span, :] = fast_rows(highs[span, :], lows[span, :], start, length, down2, gain)
            store_weights(
                queries[span, :],
                keys[pl.ds(start, tile + window), :],
                start,
                length,
                linked,
                weights.at[place // tile],
            )


def start_values(_, tail_v, own_v, values):
    window = tail_v.shape[0]
    values[0:window, :] = tail_v[...]
    join(1, window, own_v, [], values)


def mix_sent(count, weights, normed, _, *refs):
    got_v, values, outs = refs[: count - 1], refs[count - 1], refs[count:]
    rows = got_v[0].shape[0]
    tile, span = weights.shape[1:]
    head = lax.axis_index("head")
    for s in range(1, count):
        source = lax.rem(head + count - s, count)
        start = span - tile + source * rows
        values[pl.ds(pl.multiple_of(start, rows), rows), :] = got_v[s - 1][...]
    for s in range(1, count):
        device = lax.rem(head + s, count)
        for t in range(rows // tile):
            place = (s - 1) * rows + t * tile
            start = pl.multiple_of(device * rows + t * tile, tile)
            attended = dot(weights[place // tile], values[pl.ds(start, span), :])
            outs[s - 1][t * tile : (t + 1) * tile, :] = (
                attended + normed[place : place + tile, :]
            ).astype(bf16)


def renormed(old_weight, gradient, axis):
    new_weight = old_weight - gradient
    old_square = jnp.mean(old_weight * old_weight, axis=axis, keepdims=True) + epsilon
    new_square = jnp.mean(new_weight * new_weight, axis=axis, keepdims=True) + epsilon
    return new_weight * (jnp.sqrt(old_square) / jnp.sqrt(new_square))


def own_rows_and_update(
    tile,
    flags,
    gate2,
    up2,
    down2,
    gain,
    own_q,
    keys,
    values,
    turned2,
    turned,
    down,
    rate_row,
    mixed,
    new_gu,
    new_dn,
    weights,
    own,
    steps,
    gu,
    dn,
    sems,
):
    rows, width = own_q.shape
    hidden = down.shape[0]
    window = weights.shape[2] - tile
    total = keys.shape[0] - window
    linked = flags[0] == 1
    length = flags[1]
    head = lax.axis_index("head")
    for t in range(rows // tile):
        start = pl.multiple_of(head * rows + t * tile, tile)
        block = own_q[t * tile : (t + 1) * tile, :]
        high, low = hidden_rows(block, gate2, up2)
        normed = fast_rows(high, low, start, length, down2, gain)
        store_weights(
            block, keys[pl.ds(start, tile + window), :], start, length, linked, weights.at[t]
        )
        attended = dot(weights[t], values[pl.ds(start, tile + window), :])
        own[t * tile : (t + 1) * tile, :] = (attended + normed).astype(bf16)
    out_copy = pltpu.make_async_copy(own, mixed.at[0, :, head_columns(head, width)], sems.at[0])
    out_copy.start()
    ones = jnp.ones((8, 2 * width), bf16)
    step = min(256, total)
    for start in range(0, total, step):
        block_k = keys[window + start : window + start + step, :]
        block_v = values[window + start : window + start + step, :]
        block32 = block_k.astype(f32)
        square = jnp.concatenate(halves(block32 * block32), axis=1)
        unit = lax.rsqrt(dot_nt(ones, square)[:1] * (1.0 / width) + epsilon)
        rate = rate_row[:, start : start + step]
        both = dot_nt(turned2[...], wide(block_k))
        gate = both[:hidden] * unit
        up = both[hidden:] * unit
        share = sigmoid(gate)
        act = gate * share
        hidden_grad = dot_nt(down2[...], wide(block_v)) * (rate * unit)
        part = slice(start, start + step)
        steps[0:hidden, part] = (hidden_grad * up * (share + act * (1.0 - share))).astype(bf16)
        steps[hidden : 2 * hidden, part] = (hidden_grad * act).astype(bf16)
        steps[2 * hidden : 3 * hidden, part] = (act * up * rate).astype(bf16)
    both = dot(steps[0 : 2 * hidden, :], keys[window:, :])
    for index in range(2):
        part = slice(index * hidden, (index + 1) * hidden)
        gu[index] = renormed(turned[part], both[part], 1).T
    first = pltpu.make_async_copy(gu, new_gu.at[0, 0], sems.at[1])
    first.start()
    dn[...] = renormed(down[...], dot(steps[2 * hidden :, :], values[window:, :]), 0)
    second = pltpu.make_async_copy(dn, new_dn.at[0, 0], sems.at[2])
    second.start()
    out_copy.wait()
    first.wait()
    second.wait()


def place_received(count, *refs):
    got = refs[1:count]
    mixed, sems = refs[count:]
    width = got[0].shape[1]
    head = lax.axis_index("head")
    run_copies(
        [
            (got[s - 1], mixed.at[0, :, head_columns(lax.rem(head + count - s, count), width)])
            for s in range(1, count)
        ],
        sems,
    )


def params():
    return pltpu.CompilerParams(vmem_limit_bytes=24 * 1024 * 1024)


def call(body, name, outs, ins, scratch=(), cost=1, aliases={}):
    spec = {local: in_vmem, in_main: in_hbm, scalars: in_smem}
    return pl.pallas_call(
        body,
        out_shape=[shape for _, shape in outs],
        in_specs=[spec[where] for where, _ in ins],
        out_specs=[spec[where] for where, _ in outs],
        scratch_shapes=list(scratch),
        input_output_aliases=aliases,
        compiler_params=params(),
        cost_estimate=pl.CostEstimate(
            flops=int(cost * 1e6), bytes_accessed=1024, transcendentals=0
        ),
        name=name,
    )(*[where(array) for where, array in ins])


def on_device(
    queries,
    keys,
    values,
    rates,
    tail_keys,
    tail_values,
    state_in_gu,
    state_in_down,
    fresh_gu,
    fresh_down,
    out_gain,
    seq_ids,
    live_lengths,
):
    count = lax.axis_size("head")
    rows = queries.shape[1]
    width = queries.shape[2] // count
    window = tail_keys.shape[0]
    hidden = state_in_down.shape[2]
    total = rows * count
    sent = total - rows
    tile = min(256, rows)
    span = tile + window
    shifts = range(1, count)
    dma = pltpu.SemaphoreType.DMA

    def on_chip(shape, kind):
        return (local, VMEM(shape, kind))

    def in_hbm_out(shape, kind):
        return (in_main, jax.ShapeDtypeStruct(shape, kind))

    def all_local(*arrays):
        return [(local, array) for array in arrays]

    piece = on_chip((rows, width), bf16)

    got_gu = from_behind(state_in_gu[0, 0].reshape(2 * width, hidden), "ctx", 1)
    down_keys, last_v, *packed = call(
        functools.partial(pack, count),
        "pack",
        [on_chip((2 * hidden + window, width), bf16), on_chip((window, width), bf16)]
        + [on_chip((2 * rows, width), bf16)] * (count - 1)
        + [piece] * (count - 1),
        [
            (in_main, array)
            for array in (queries, keys, values, state_in_down, tail_keys, tail_values)
        ],
        scratch=[VMEM((hidden, width), f32), dma((3 * count,))],
    )
    sent_qk, sent_v = packed[: count - 1], packed[count - 1 :]
    got_qk = [from_behind(sent_qk[s - 1], "head", s) for s in shifts]
    got_dk = from_behind(down_keys, "ctx", 1)
    prior_v = from_behind(last_v, "ctx", 1)
    got_v = [from_behind(sent_v[s - 1], "head", s) for s in shifts]

    own_q, own_k, own_v, fresh, gain, rate_row, flags = call(
        functools.partial(load, count),
        "load",
        [
            piece,
            piece,
            piece,
            on_chip((3 * width, hidden), f32),
            on_chip((1, width), f32),
            on_chip((1, total), f32),
            (scalars, pltpu.SMEM((2,), jnp.int32)),
        ],
        [
            (in_main, array)
            for array in (
                queries,
                keys,
                values,
                fresh_gu,
                fresh_down,
                out_gain[None],
                rates,
                seq_ids.T,
                live_lengths.T,
            )
        ]
        + all_local(sent_qk[0]),
        scratch=[
            pltpu.SMEM(seq_ids.shape[::-1], jnp.int32),
            pltpu.SMEM(live_lengths.shape[::-1], jnp.int32),
            dma((9 + hidden // width,)),
        ],
    )
    gate2, up2, turned2, turned, live_rates = call(
        choose_gate_up,
        "choose_gate_up",
        [
            on_chip((2 * width, hidden), bf16),
            on_chip((2 * width, hidden), bf16),
            on_chip((2 * hidden, 2 * width), bf16),
            on_chip((2 * hidden, width), f32),
            on_chip((1, total), f32),
        ],
        [(scalars, flags)] + all_local(got_gu, fresh, rate_row),
        cost=500,
    )
    all_keys_shape = on_chip((window + total, width), bf16)
    sent_q, highs, lows, all_keys = call(
        functools.partial(sent_hidden, count, tile, window),
        "sent_hidden",
        [on_chip((sent, width), bf16)]
        + [on_chip((sent, hidden), bf16)] * 2
        + [all_keys_shape],
        all_local(gate2, up2, own_k, *got_qk),
        cost=500,
    )
    down2, down, all_keys = call(
        choose_down,
        "choose_down",
        [on_chip((hidden, 2 * width), bf16), on_chip((hidden, width), f32), all_keys_shape],
        [(scalars, flags)] + all_local(got_dk, fresh, all_keys),
        aliases={3: 2},
    )
    weights, normed = call(
        functools.partial(sent_rows, count, tile),
        "sent_rows",
        [on_chip((sent // tile, tile, span), bf16), on_chip((sent, width), f32)],
        [(scalars, flags)] + all_local(down2, gain, all_keys, sent_q, highs, lows),
        cost=1,
    )
    (all_values,) = call(
        start_values,
        "start_values",
        [on_chip((window + total, width), bf16)],
        all_local(normed, prior_v, own_v),
        cost=1,
    )
    all_values, *mixed_out = call(
        functools.partial(mix_sent, count),
        "mix_sent",
        [on_chip((window + total, width), bf16)] + [piece] * (count - 1),
        all_local(weights, normed, all_values, *got_v),
        aliases={2: 0},
    )
    mixed_in = [from_behind(mixed_out[s - 1], "head", s) for s in shifts]
    mixed, new_gu, new_down = call(
        functools.partial(own_rows_and_update, tile),
        "own_rows_and_update",
        [
            in_hbm_out(queries.shape, bf16),
            in_hbm_out(state_in_gu.shape, f32),
            in_hbm_out(state_in_down.shape, f32),
        ],
        [(scalars, flags)]
        + all_local(
            gate2, up2, down2, gain, own_q, all_keys, all_values, turned2, turned, down, live_rates
        ),
        scratch=[
            VMEM((rows // tile, tile, span), bf16),
            VMEM((rows, width), bf16),
            VMEM((3 * hidden, total), bf16),
            VMEM(state_in_gu.shape[2:], f32),
            VMEM(state_in_down.shape[2:], f32),
            dma((3,)),
        ],
    )
    (mixed,) = call(
        functools.partial(place_received, count),
        "place_received",
        [in_hbm_out(queries.shape, bf16)],
        [(in_main, mixed)] + all_local(*mixed_in),
        scratch=[dma((count - 1,))],
        aliases={0: 0},
    )
    return (mixed, new_gu, new_down)


def solution(mesh):
    placed = (
        P(None, ("ctx", "head"), None),
        P(None, ("ctx", "head"), None),
        P(None, ("ctx", "head"), None),
        P(None, "head", "ctx"),
        P("ctx", "head"),
        P("ctx", "head"),
        P("ctx", "head", None, None, None),
        P("ctx", "head", None, None),
        P("head", None, None, None),
        P("head", None, None),
        P("head"),
        P(),
        P(),
    )
    return jax.shard_map(
        on_device,
        mesh=mesh,
        in_specs=placed,
        out_specs=(
            P(None, ("ctx", "head"), None),
            P("ctx", "head", None, None, None),
            P("ctx", "head", None, None),
        ),
        check_vma=False,
    )
```

```python
import functools
import math

import jax
import jax.numpy as jnp
from jax import lax
from jax.experimental import pallas as pl
from jax.experimental.pallas import tpu as pltpu
from jax.sharding import PartitionSpec as P

epsilon = 1e-06
masked = -1e30
f32 = jnp.float32
bf16 = jnp.bfloat16

VMEM = pltpu.VMEM
in_vmem = pl.BlockSpec(memory_space=pltpu.VMEM)
in_smem = pl.BlockSpec(memory_space=pltpu.SMEM)
in_hbm = pl.BlockSpec(memory_space=pltpu.HBM)


def from_behind(shard, axis, by):
    size = lax.axis_size(axis)
    return lax.ppermute(shard, axis, [(i, (i + by) % size) for i in range(size)])


def local(array):
    return pltpu.with_memory_space_constraint(array, pltpu.VMEM)


def in_main(array):
    return pltpu.with_memory_space_constraint(array, pltpu.HBM)


def scalars(array):
    return pltpu.with_memory_space_constraint(array, pltpu.SMEM)


def run_copies(pairs, sems):
    copies = [
        pltpu.make_async_copy(source, target, sems.at[i]) for i, (source, target) in enumerate(pairs)
    ]
    for copy in copies:
        copy.start()
    for copy in copies:
        copy.wait()


def head_columns(index, width):
    return pl.ds(pl.multiple_of(index * width, width), width)


def wide(array):
    return jnp.concatenate([array, array], axis=1)


def halves(array):
    high = array.astype(bf16)
    low = (array - high.astype(f32)).astype(bf16)
    return high, low


def dot(left, right):
    return jnp.dot(left, right, preferred_element_type=f32)


def dot_nt(left, right):
    return lax.dot_general(left, right, (((1,), (1,)), ((), ())), preferred_element_type=f32)


def sigmoid(x):
    return 0.5 * jnp.tanh(0.5 * x) + 0.5


def row_block(index, rows):
    return pl.ds(pl.multiple_of(index * rows, rows), rows)


def fast_rows(high, low, first_row, length, down2, gain):
    count = high.shape[0]
    width = down2.shape[1] // 2
    both = dot(high, down2[...])
    fast = both[:, :width] + both[:, width:] + dot(low, down2[:, :width])
    scale = lax.rsqrt(jnp.mean(fast * fast, axis=-1, keepdims=True) + epsilon)
    row = first_row + lax.broadcasted_iota(jnp.int32, (count, 1), 0)
    return fast * jnp.where(row < length, scale, 0.0) * gain[...]


def store_weights(queries, keys, first_row, length, linked, out):
    tile, width = queries.shape
    window = keys.shape[0] - tile
    place = first_row - window + lax.broadcasted_iota(jnp.int32, (1, tile + window), 1)
    bias = jnp.where((place < length) & ((place >= 0) | linked), 0.0, masked)
    row = lax.broadcasted_iota(jnp.int32, (tile, tile), 0)
    column = lax.broadcasted_iota(jnp.int32, (tile, tile), 1)
    later = column > row
    factor = math.log2(math.e) / math.sqrt(width)
    scores = dot_nt(queries, keys) * factor
    first = jnp.where(later, scores[:, :tile] + bias[:, :tile], masked)
    last = scores[:, window:]
    last = jnp.where(column == row, last, last + bias[:, window:])
    last = jnp.where(later, masked, last)
    parts = [(0, first), (window, last)]
    if tile < window:
        parts.append((tile, scores[:, tile:window] + bias[:, tile:window]))
    largest = functools.reduce(
        jnp.maximum, [jnp.max(part, axis=-1, keepdims=True) for _, part in parts]
    )
    parts = [(offset, jnp.exp2(part - largest)) for offset, part in parts]
    total = sum(jnp.sum(part, axis=-1, keepdims=True) for _, part in parts)
    token = first_row + lax.broadcasted_iota(jnp.int32, (tile, 1), 0)
    scale = jnp.where(token < length, 1.0 / total, 0.0)
    for offset, part in parts:
        out[:, offset : offset + part.shape[1]] = (part * scale).astype(bf16)


def join(count, window, own, got, joined):
    rows = own.shape[0]
    head = lax.axis_index("head")
    joined[pl.ds(pl.multiple_of(window + head * rows, rows), rows), :] = own[...]
    for s in range(1, count):
        source = lax.rem(head + count - s, count)
        joined[pl.ds(pl.multiple_of(window + source * rows, rows), rows), :] = got[s - 1][...]


def pack(count, q_ref, k_ref, v_ref, dn_ref, tail_k, tail_v, *refs):
    down_keys, last_v = refs[:2]
    sent_qk, sent_v = refs[2 : 1 + count], refs[1 + count : 2 * count]
    down, sems = refs[-2:]
    head = lax.axis_index("head")
    hidden, width = down.shape
    rows = sent_v[0].shape[0]
    pairs = [(dn_ref.at[0, 0], down)]
    for s in range(1, count):
        columns = head_columns(lax.rem(head + s, count), width)
        pairs.append((q_ref.at[0, :, columns], sent_qk[s - 1].at[0:rows]))
        pairs.append((k_ref.at[0, :, columns], sent_qk[s - 1].at[rows : 2 * rows]))
        pairs.append((v_ref.at[0, :, columns], sent_v[s - 1]))
    pairs += [(tail_k, down_keys.at[2 * hidden :]), (tail_v, last_v)]
    run_copies(pairs, sems)
    high, low = halves(down[...])
    down_keys[0:hidden] = high
    down_keys[hidden : 2 * hidden] = low


def load(
    count, q_ref, k_ref, v_ref, fresh_gu, fresh_dn, gain, rates, ids_ref, len_ref, _, own_q, own_k,
    own_v, fresh,
    gain_row, rate_row, flags, ids, lens, sems
):
    head = lax.axis_index("head")
    here = lax.axis_index("ctx")
    width = own_k.shape[1]
    columns = head_columns(head, width)
    pairs = [
        (q_ref.at[0, :, columns], own_q),
        (k_ref.at[0, :, columns], own_k),
        (v_ref.at[0, :, columns], own_v),
        (fresh_gu.at[0, 0], fresh.at[0:width]),
        (fresh_gu.at[0, 1], fresh.at[width : 2 * width]),
    ]
    for group in range(fresh_dn.shape[1] // width):
        part = slice(group * width, (group + 1) * width)
        pairs.append((fresh_dn.at[0, part], fresh.at[2 * width : 3 * width, part]))
    pairs += [(gain, gain_row), (rates.at[0], rate_row), (ids_ref, ids), (len_ref, lens)]
    run_copies(pairs, sems)
    size = ids.shape[1]
    before = lax.rem(here + size - 1, size)
    flags[0] = (ids[1, here] == ids[0, before]).astype(jnp.int32)
    flags[1] = lens[0, here]


def hidden_rows(queries, gate2, up2):
    queries32 = queries.astype(f32)
    unit = lax.rsqrt(jnp.mean(queries32 * queries32, axis=-1, keepdims=True) + epsilon)
    doubled = wide(queries)
    gate = dot(doubled, gate2[...]) * unit
    up = dot(doubled, up2[...]) * unit
    return halves(gate * sigmoid(gate) * up)


def query_hidden(count, tile, window, gate2, up2, own_q, own_k, *refs):
    got_qk, (queries, highs, lows, keys) = refs[: count - 1], refs[count - 1 :]
    rows, width = own_k.shape
    for s in range(1, count + 1):
        source = own_q if s == count else got_qk[count - s - 1]
        for t in range(rows // tile):
            span = slice((s - 1) * rows + t * tile, (s - 1) * rows + (t + 1) * tile)
            block = source[t * tile : (t + 1) * tile, :]
            queries[span, :] = block
            high, low = hidden_rows(block, gate2, up2)
            highs[span, :] = high
            lows[span, :] = low
    join(count, window, own_k, [got.at[rows : 2 * rows] for got in got_qk], keys)


def choose_gate_up(flags, got_gu, fresh, rates, gate2, up2, turned2, turned, rate_row):
    hidden = fresh.shape[1]
    width = got_gu.shape[0] // 2
    linked = flags[0] == 1
    length = flags[1]
    for index, split in enumerate((gate2, up2)):
        rows = slice(index * width, (index + 1) * width)
        weight = jnp.where(linked, got_gu[rows], fresh[rows])
        split[...] = jnp.concatenate(halves(weight), axis=0)
        part = slice(index * hidden, (index + 1) * hidden)
        weight = weight.T
        turned[part] = weight
        turned2[part] = jnp.concatenate(halves(weight), axis=1)
    token = lax.broadcasted_iota(jnp.int32, rates.shape, 1)
    rate_row[...] = jnp.where(token < length, -rates[...], 0.0)


def choose_down(flags, down_keys, fresh, keys, down2, down, joined):
    hidden, width = down.shape
    window = down_keys.shape[0] - 2 * hidden
    linked = flags[0] == 1
    fresh_down = jnp.concatenate(
        [fresh[2 * width :, g * width : (g + 1) * width] for g in range(hidden // width)], axis=0
    )
    got_down = down_keys[0:hidden].astype(f32) + down_keys[hidden : 2 * hidden].astype(f32)
    w_down = jnp.where(linked, got_down, fresh_down)
    down[...] = w_down
    down2[...] = jnp.concatenate(halves(w_down), axis=1)
    joined[0:window] = down_keys[2 * hidden :]


def sent_rows(count, tile, flags, down2, gain, keys, queries, highs, lows, weights, normed):
    rows = queries.shape[0] // count
    window = keys.shape[0] - count * rows
    linked = flags[0] == 1
    length = flags[1]
    head = lax.axis_index("head")
    for s in range(1, count):
        device = lax.rem(head + s, count)
        for t in range(rows // tile):
            place = (s - 1) * rows + t * tile
            start = pl.multiple_of(device * rows + t * tile, tile)
            span = slice(place, place + tile)
            normed[span, :] = fast_rows(highs[span, :], lows[span, :], start, length, down2, gain)
            store_weights(
                queries[span, :],
                keys[pl.ds(start, tile + window), :],
                start,
                length,
                linked,
                weights.at[place // tile],
            )


def start_values(_, tail_v, own_v, values):
    window = tail_v.shape[0]
    values[0:window, :] = tail_v[...]
    join(1, window, own_v, [], values)


def mix_sent(count, weights, normed, _, *refs):
    got_v, values, outs = refs[: count - 1], refs[count - 1], refs[count:]
    rows = got_v[0].shape[0]
    tile, span = weights.shape[1:]
    head = lax.axis_index("head")
    for s in range(1, count):
        source = lax.rem(head + count - s, count)
        start = span - tile + source * rows
        values[pl.ds(pl.multiple_of(start, rows), rows), :] = got_v[s - 1][...]
    for s in range(1, count):
        device = lax.rem(head + s, count)
        for t in range(rows // tile):
            place = (s - 1) * rows + t * tile
            start = pl.multiple_of(device * rows + t * tile, tile)
            attended = dot(weights[place // tile], values[pl.ds(start, span), :])
            outs[s - 1][t * tile : (t + 1) * tile, :] = (
                attended + normed[place : place + tile, :]
            ).astype(bf16)


def renormed(old_weight, gradient, axis):
    new_weight = old_weight - gradient
    old_square = jnp.mean(old_weight * old_weight, axis=axis, keepdims=True) + epsilon
    new_square = jnp.mean(new_weight * new_weight, axis=axis, keepdims=True) + epsilon
    return new_weight * (jnp.sqrt(old_square) / jnp.sqrt(new_square))


def own_rows_and_update(
    tile,
    flags,
    down2,
    gain,
    queries,
    highs,
    lows,
    keys,
    values,
    turned2,
    turned,
    down,
    rate_row,
    mixed,
    new_gu,
    new_dn,
    weights,
    own,
    steps,
    gu,
    dn,
    sems,
):
    rows, width = own.shape
    hidden = down.shape[0]
    window = weights.shape[2] - tile
    total = keys.shape[0] - window
    linked = flags[0] == 1
    length = flags[1]
    head = lax.axis_index("head")
    for t in range(rows // tile):
        start = pl.multiple_of(head * rows + t * tile, tile)
        place = total - rows + t * tile
        span = slice(place, place + tile)
        normed = fast_rows(highs[span, :], lows[span, :], start, length, down2, gain)
        keys_here = keys[pl.ds(start, tile + window), :]
        store_weights(queries[span, :], keys_here, start, length, linked, weights.at[t])
        attended = dot(weights[t], values[pl.ds(start, tile + window), :])
        own[t * tile : (t + 1) * tile, :] = (attended + normed).astype(bf16)
    out_copy = pltpu.make_async_copy(own, mixed.at[0, :, head_columns(head, width)], sems.at[0])
    out_copy.start()
    ones = jnp.ones((8, 2 * width), bf16)
    step = min(256, total)
    for start in range(0, total, step):
        block_k = keys[window + start : window + start + step, :]
        block_v = values[window + start : window + start + step, :]
        block32 = block_k.astype(f32)
        square = jnp.concatenate(halves(block32 * block32), axis=1)
        unit = lax.rsqrt(dot_nt(ones, square)[:1] * (1.0 / width) + epsilon)
        rate = rate_row[:, start : start + step]
        both = dot_nt(turned2[...], wide(block_k))
        gate = both[:hidden] * unit
        up = both[hidden:] * unit
        share = sigmoid(gate)
        act = gate * share
        hidden_grad = dot_nt(down2[...], wide(block_v)) * (rate * unit)
        part = slice(start, start + step)
        steps[0:hidden, part] = (hidden_grad * up * (share + act * (1.0 - share))).astype(bf16)
        steps[hidden : 2 * hidden, part] = (hidden_grad * act).astype(bf16)
        steps[2 * hidden : 3 * hidden, part] = (act * up * rate).astype(bf16)
    both = dot(steps[0 : 2 * hidden, :], keys[window:, :])
    for index in range(2):
        part = slice(index * hidden, (index + 1) * hidden)
        gu[index] = renormed(turned[part], both[part], 1).T
    first = pltpu.make_async_copy(gu, new_gu.at[0, 0], sems.at[1])
    first.start()
    dn[...] = renormed(down[...], dot(steps[2 * hidden :, :], values[window:, :]), 0)
    second = pltpu.make_async_copy(dn, new_dn.at[0, 0], sems.at[2])
    second.start()
    out_copy.wait()
    first.wait()
    second.wait()


def place_received(count, *refs):
    got = refs[1:count]
    mixed, sems = refs[count:]
    width = got[0].shape[1]
    head = lax.axis_index("head")
    run_copies(
        [
            (got[s - 1], mixed.at[0, :, head_columns(lax.rem(head + count - s, count), width)])
            for s in range(1, count)
        ],
        sems,
    )


def params():
    return pltpu.CompilerParams(vmem_limit_bytes=24 * 1024 * 1024)


def call(body, name, outs, ins, scratch=(), cost=1, aliases={}):
    spec = {local: in_vmem, in_main: in_hbm, scalars: in_smem}
    return pl.pallas_call(
        body,
        out_shape=[shape for _, shape in outs],
        in_specs=[spec[where] for where, _ in ins],
        out_specs=[spec[where] for where, _ in outs],
        scratch_shapes=list(scratch),
        input_output_aliases=aliases,
        compiler_params=params(),
        cost_estimate=pl.CostEstimate(
            flops=int(cost * 1e6), bytes_accessed=1024, transcendentals=0
        ),
        name=name,
    )(*[where(array) for where, array in ins])


def on_device(
    queries,
    keys,
    values,
    rates,
    tail_keys,
    tail_values,
    state_in_gu,
    state_in_down,
    fresh_gu,
    fresh_down,
    out_gain,
    seq_ids,
    live_lengths,
):
    count = lax.axis_size("head")
    rows = queries.shape[1]
    width = queries.shape[2] // count
    window = tail_keys.shape[0]
    hidden = state_in_down.shape[2]
    total = rows * count
    sent = total - rows
    tile = min(256, rows)
    span = tile + window
    shifts = range(1, count)
    dma = pltpu.SemaphoreType.DMA

    def on_chip(shape, kind):
        return (local, VMEM(shape, kind))

    def in_hbm_out(shape, kind):
        return (in_main, jax.ShapeDtypeStruct(shape, kind))

    def all_local(*arrays):
        return [(local, array) for array in arrays]

    piece = on_chip((rows, width), bf16)

    got_gu = from_behind(state_in_gu[0, 0].reshape(2 * width, hidden), "ctx", 1)
    down_keys, last_v, *packed = call(
        functools.partial(pack, count),
        "pack",
        [on_chip((2 * hidden + window, width), bf16), on_chip((window, width), bf16)]
        + [on_chip((2 * rows, width), bf16)] * (count - 1)
        + [piece] * (count - 1),
        [
            (in_main, array)
            for array in (queries, keys, values, state_in_down, tail_keys, tail_values)
        ],
        scratch=[VMEM((hidden, width), f32), dma((3 * count,))],
    )
    sent_qk, sent_v = packed[: count - 1], packed[count - 1 :]
    got_qk = [from_behind(sent_qk[s - 1], "head", s) for s in shifts]
    got_dk = from_behind(down_keys, "ctx", 1)
    prior_v = from_behind(last_v, "ctx", 1)

    own_q, own_k, own_v, fresh, gain, rate_row, flags = call(
        functools.partial(load, count),
        "load",
        [
            piece,
            piece,
            piece,
            on_chip((3 * width, hidden), f32),
            on_chip((1, width), f32),
            on_chip((1, total), f32),
            (scalars, pltpu.SMEM((2,), jnp.int32)),
        ],
        [
            (in_main, array)
            for array in (
                queries,
                keys,
                values,
                fresh_gu,
                fresh_down,
                out_gain[None],
                rates,
                seq_ids.T,
                live_lengths.T,
            )
        ]
        + all_local(sent_qk[0]),
        scratch=[
            pltpu.SMEM(seq_ids.shape[::-1], jnp.int32),
            pltpu.SMEM(live_lengths.shape[::-1], jnp.int32),
            dma((9 + hidden // width,)),
        ],
    )
    held_v = lax.optimization_barrier((fresh, *sent_v))[1:]
    got_v = [from_behind(held_v[s - 1], "head", s) for s in shifts]
    gate2, up2, turned2, turned, live_rates = call(
        choose_gate_up,
        "choose_gate_up",
        [
            on_chip((2 * width, hidden), bf16),
            on_chip((2 * width, hidden), bf16),
            on_chip((2 * hidden, 2 * width), bf16),
            on_chip((2 * hidden, width), f32),
            on_chip((1, total), f32),
        ],
        [(scalars, flags)] + all_local(got_gu, fresh, rate_row),
        cost=500,
    )
    all_keys_shape = on_chip((window + total, width), bf16)
    all_q, highs, lows, all_keys = call(
        functools.partial(query_hidden, count, tile, window),
        "query_hidden",
        [on_chip((total, width), bf16)]
        + [on_chip((total, hidden), bf16)] * 2
        + [all_keys_shape],
        all_local(gate2, up2, own_q, own_k, *got_qk),
        cost=500,
    )
    down2, down, all_keys = call(
        choose_down,
        "choose_down",
        [on_chip((hidden, 2 * width), bf16), on_chip((hidden, width), f32), all_keys_shape],
        [(scalars, flags)] + all_local(got_dk, fresh, all_keys),
        aliases={3: 2},
    )
    weights, normed = call(
        functools.partial(sent_rows, count, tile),
        "sent_rows",
        [on_chip((sent // tile, tile, span), bf16), on_chip((sent, width), f32)],
        [(scalars, flags)] + all_local(down2, gain, all_keys, all_q, highs, lows),
        cost=1,
    )
    (all_values,) = call(
        start_values,
        "start_values",
        [on_chip((window + total, width), bf16)],
        all_local(normed, prior_v, own_v),
        cost=1,
    )
    all_values, *mixed_out = call(
        functools.partial(mix_sent, count),
        "mix_sent",
        [on_chip((window + total, width), bf16)] + [piece] * (count - 1),
        all_local(weights, normed, all_values, *got_v),
        aliases={2: 0},
    )
    mixed_in = [from_behind(mixed_out[s - 1], "head", s) for s in shifts]
    mixed, new_gu, new_down = call(
        functools.partial(own_rows_and_update, tile),
        "own_rows_and_update",
        [
            in_hbm_out(queries.shape, bf16),
            in_hbm_out(state_in_gu.shape, f32),
            in_hbm_out(state_in_down.shape, f32),
        ],
        [(scalars, flags)]
        + all_local(
            down2,
            gain,
            all_q,
            highs,
            lows,
            all_keys,
            all_values,
            turned2,
            turned,
            down,
            live_rates,
        ),
        scratch=[
            VMEM((rows // tile, tile, span), bf16),
            VMEM((rows, width), bf16),
            VMEM((3 * hidden, total), bf16),
            VMEM(state_in_gu.shape[2:], f32),
            VMEM(state_in_down.shape[2:], f32),
            dma((3,)),
        ],
    )
    (mixed,) = call(
        functools.partial(place_received, count),
        "place_received",
        [in_hbm_out(queries.shape, bf16)],
        [(in_main, mixed)] + all_local(*mixed_in),
        scratch=[dma((count - 1,))],
        aliases={0: 0},
    )
    return (mixed, new_gu, new_down)


def solution(mesh):
    placed = (
        P(None, ("ctx", "head"), None),
        P(None, ("ctx", "head"), None),
        P(None, ("ctx", "head"), None),
        P(None, "head", "ctx"),
        P("ctx", "head"),
        P("ctx", "head"),
        P("ctx", "head", None, None, None),
        P("ctx", "head", None, None),
        P("head", None, None, None),
        P("head", None, None),
        P("head"),
        P(),
        P(),
    )
    return jax.shard_map(
        on_device,
        mesh=mesh,
        in_specs=placed,
        out_specs=(
            P(None, ("ctx", "head"), None),
            P("ctx", "head", None, None, None),
            P("ctx", "head", None, None),
        ),
        check_vma=False,
    )
```

```python
import functools
import math

import jax
import jax.numpy as jnp
from jax import lax
from jax.experimental import pallas as pl
from jax.experimental.pallas import tpu as pltpu
from jax.sharding import PartitionSpec as P

epsilon = 1e-06
masked = -1e30
f32 = jnp.float32
bf16 = jnp.bfloat16

VMEM = pltpu.VMEM
in_vmem = pl.BlockSpec(memory_space=pltpu.VMEM)
in_smem = pl.BlockSpec(memory_space=pltpu.SMEM)
in_hbm = pl.BlockSpec(memory_space=pltpu.HBM)


def from_behind(shard, axis, by):
    size = lax.axis_size(axis)
    return lax.ppermute(shard, axis, [(i, (i + by) % size) for i in range(size)])


def local(array):
    return pltpu.with_memory_space_constraint(array, pltpu.VMEM)


def in_main(array):
    return pltpu.with_memory_space_constraint(array, pltpu.HBM)


def scalars(array):
    return pltpu.with_memory_space_constraint(array, pltpu.SMEM)


def run_copies(pairs, sems):
    copies = [
        pltpu.make_async_copy(source, target, sems.at[i]) for i, (source, target) in enumerate(pairs)
    ]
    for copy in copies:
        copy.start()
    for copy in copies:
        copy.wait()


def head_columns(index, width):
    return pl.ds(pl.multiple_of(index * width, width), width)


def wide(array):
    return jnp.concatenate([array, array], axis=1)


def halves(array):
    high = array.astype(bf16)
    low = (array - high.astype(f32)).astype(bf16)
    return high, low


def dot(left, right):
    return jnp.dot(left, right, preferred_element_type=f32)


def dot_nt(left, right):
    return lax.dot_general(left, right, (((1,), (1,)), ((), ())), preferred_element_type=f32)


def sigmoid(x):
    return 0.5 * jnp.tanh(0.5 * x) + 0.5


def row_block(index, rows):
    return pl.ds(pl.multiple_of(index * rows, rows), rows)


def fast_rows(high, low, first_row, length, down2, gain):
    count = high.shape[0]
    width = down2.shape[1] // 2
    both = dot(high, down2[...])
    fast = both[:, :width] + both[:, width:] + dot(low, down2[:, :width])
    scale = lax.rsqrt(jnp.mean(fast * fast, axis=-1, keepdims=True) + epsilon)
    row = first_row + lax.broadcasted_iota(jnp.int32, (count, 1), 0)
    return fast * jnp.where(row < length, scale, 0.0) * gain[...]


def store_weights(queries, keys, first_row, length, linked, out):
    tile, width = queries.shape
    window = keys.shape[0] - tile
    place = first_row - window + lax.broadcasted_iota(jnp.int32, (1, tile + window), 1)
    bias = jnp.where((place < length) & ((place >= 0) | linked), 0.0, masked)
    row = lax.broadcasted_iota(jnp.int32, (tile, tile), 0)
    column = lax.broadcasted_iota(jnp.int32, (tile, tile), 1)
    later = column > row
    factor = math.log2(math.e) / math.sqrt(width)
    scores = dot_nt(queries, keys) * factor
    first = jnp.where(later, scores[:, :tile] + bias[:, :tile], masked)
    last = scores[:, window:]
    last = jnp.where(column == row, last, last + bias[:, window:])
    last = jnp.where(later, masked, last)
    parts = [(0, first), (window, last)]
    if tile < window:
        parts.append((tile, scores[:, tile:window] + bias[:, tile:window]))
    largest = functools.reduce(
        jnp.maximum, [jnp.max(part, axis=-1, keepdims=True) for _, part in parts]
    )
    parts = [(offset, jnp.exp2(part - largest)) for offset, part in parts]
    total = sum(jnp.sum(part, axis=-1, keepdims=True) for _, part in parts)
    token = first_row + lax.broadcasted_iota(jnp.int32, (tile, 1), 0)
    scale = jnp.where(token < length, 1.0 / total, 0.0)
    for offset, part in parts:
        out[:, offset : offset + part.shape[1]] = (part * scale).astype(bf16)


def join(count, window, own, got, joined):
    rows = own.shape[0]
    head = lax.axis_index("head")
    joined[pl.ds(pl.multiple_of(window + head * rows, rows), rows), :] = own[...]
    for s in range(1, count):
        source = lax.rem(head + count - s, count)
        joined[pl.ds(pl.multiple_of(window + source * rows, rows), rows), :] = got[s - 1][...]


def pack(count, q_ref, k_ref, v_ref, dn_ref, tail_k, tail_v, *refs):
    down_keys, last_v = refs[:2]
    sent_qk, sent_v = refs[2 : 1 + count], refs[1 + count : 2 * count]
    down, sems = refs[-2:]
    head = lax.axis_index("head")
    hidden, width = down.shape
    rows = sent_v[0].shape[0]
    pairs = [(dn_ref.at[0, 0], down)]
    for s in range(1, count):
        columns = head_columns(lax.rem(head + s, count), width)
        pairs.append((q_ref.at[0, :, columns], sent_qk[s - 1].at[0:rows]))
        pairs.append((k_ref.at[0, :, columns], sent_qk[s - 1].at[rows : 2 * rows]))
        pairs.append((v_ref.at[0, :, columns], sent_v[s - 1]))
    pairs += [(tail_k, down_keys.at[2 * hidden :]), (tail_v, last_v)]
    run_copies(pairs, sems)
    high, low = halves(down[...])
    down_keys[0:hidden] = high
    down_keys[hidden : 2 * hidden] = low


def load(
    count, q_ref, k_ref, v_ref, fresh_gu, fresh_dn, gain, rates, ids_ref, len_ref, _, own_q, own_k,
    own_v, fresh,
    gain_row, rate_row, flags, ids, lens, sems
):
    head = lax.axis_index("head")
    here = lax.axis_index("ctx")
    width = own_k.shape[1]
    columns = head_columns(head, width)
    pairs = [
        (q_ref.at[0, :, columns], own_q),
        (k_ref.at[0, :, columns], own_k),
        (v_ref.at[0, :, columns], own_v),
        (fresh_gu.at[0, 0], fresh.at[0:width]),
        (fresh_gu.at[0, 1], fresh.at[width : 2 * width]),
    ]
    for group in range(fresh_dn.shape[1] // width):
        part = slice(group * width, (group + 1) * width)
        pairs.append((fresh_dn.at[0, part], fresh.at[2 * width : 3 * width, part]))
    pairs += [(gain, gain_row), (rates.at[0], rate_row), (ids_ref, ids), (len_ref, lens)]
    run_copies(pairs, sems)
    size = ids.shape[1]
    before = lax.rem(here + size - 1, size)
    flags[0] = (ids[1, here] == ids[0, before]).astype(jnp.int32)
    flags[1] = lens[0, here]


def hidden_rows(queries, gate2, up2):
    queries32 = queries.astype(f32)
    unit = lax.rsqrt(jnp.mean(queries32 * queries32, axis=-1, keepdims=True) + epsilon)
    doubled = wide(queries)
    gate = dot(doubled, gate2[...]) * unit
    up = dot(doubled, up2[...]) * unit
    return halves(gate * sigmoid(gate) * up)


def query_hidden(count, tile, window, gate2, up2, own_q, own_k, *refs):
    got_qk, (queries, highs, lows, keys) = refs[: count - 1], refs[count - 1 :]
    rows, width = own_k.shape
    for s in range(1, count + 1):
        source = own_q if s == count else got_qk[count - s - 1]
        for t in range(rows // tile):
            span = slice((s - 1) * rows + t * tile, (s - 1) * rows + (t + 1) * tile)
            block = source[t * tile : (t + 1) * tile, :]
            queries[span, :] = block
            high, low = hidden_rows(block, gate2, up2)
            highs[span, :] = high
            lows[span, :] = low
    join(count, window, own_k, [got.at[rows : 2 * rows] for got in got_qk], keys)


def choose_gate_up(flags, got_gu, fresh, rates, gate2, up2, turned2, turned, rate_row):
    hidden = fresh.shape[1]
    width = got_gu.shape[0] // 2
    linked = flags[0] == 1
    length = flags[1]
    for index, split in enumerate((gate2, up2)):
        rows = slice(index * width, (index + 1) * width)
        weight = jnp.where(linked, got_gu[rows], fresh[rows])
        split[...] = jnp.concatenate(halves(weight), axis=0)
        part = slice(index * hidden, (index + 1) * hidden)
        weight = weight.T
        turned[part] = weight
        turned2[part] = jnp.concatenate(halves(weight), axis=1)
    token = lax.broadcasted_iota(jnp.int32, rates.shape, 1)
    rate_row[...] = jnp.where(token < length, -rates[...], 0.0)


def choose_down(flags, down_keys, fresh, keys, down2, down, joined):
    hidden, width = down.shape
    window = down_keys.shape[0] - 2 * hidden
    linked = flags[0] == 1
    fresh_down = jnp.concatenate(
        [fresh[2 * width :, g * width : (g + 1) * width] for g in range(hidden // width)], axis=0
    )
    got_down = down_keys[0:hidden].astype(f32) + down_keys[hidden : 2 * hidden].astype(f32)
    w_down = jnp.where(linked, got_down, fresh_down)
    down[...] = w_down
    down2[...] = jnp.concatenate(halves(w_down), axis=1)
    joined[0:window] = down_keys[2 * hidden :]


def sent_rows(count, tile, flags, down2, gain, keys, queries, highs, lows, weights, normed):
    rows = queries.shape[0] // count
    window = keys.shape[0] - count * rows
    linked = flags[0] == 1
    length = flags[1]
    head = lax.axis_index("head")
    for s in range(1, count):
        device = lax.rem(head + s, count)
        for t in range(rows // tile):
            place = (s - 1) * rows + t * tile
            start = pl.multiple_of(device * rows + t * tile, tile)
            span = slice(place, place + tile)
            normed[span, :] = fast_rows(highs[span, :], lows[span, :], start, length, down2, gain)
            store_weights(
                queries[span, :],
                keys[pl.ds(start, tile + window), :],
                start,
                length,
                linked,
                weights.at[place // tile],
            )


def start_values(_, tail_v, own_v, values):
    window = tail_v.shape[0]
    values[0:window, :] = tail_v[...]
    join(1, window, own_v, [], values)


def mix_sent(count, weights, normed, _, *refs):
    got_v, values, outs = refs[: count - 1], refs[count - 1], refs[count:]
    rows = got_v[0].shape[0]
    tile, span = weights.shape[1:]
    head = lax.axis_index("head")
    for s in range(1, count):
        source = lax.rem(head + count - s, count)
        start = span - tile + source * rows
        values[pl.ds(pl.multiple_of(start, rows), rows), :] = got_v[s - 1][...]
    for s in range(1, count):
        device = lax.rem(head + s, count)
        for t in range(rows // tile):
            place = (s - 1) * rows + t * tile
            start = pl.multiple_of(device * rows + t * tile, tile)
            attended = dot(weights[place // tile], values[pl.ds(start, span), :])
            outs[s - 1][t * tile : (t + 1) * tile, :] = (
                attended + normed[place : place + tile, :]
            ).astype(bf16)


def renormed(old_weight, gradient, axis):
    new_weight = old_weight - gradient
    old_square = jnp.mean(old_weight * old_weight, axis=axis, keepdims=True) + epsilon
    new_square = jnp.mean(new_weight * new_weight, axis=axis, keepdims=True) + epsilon
    return new_weight * (jnp.sqrt(old_square) / jnp.sqrt(new_square))


def fill_key_parts(window, keys, turned2, rate_row, gate_part, up_part, down_steps):
    hidden, total = down_steps.shape
    width = keys.shape[1]
    ones = jnp.ones((8, 2 * width), bf16)
    step = min(256, total)
    for start in range(0, total, step):
        block = keys[window + start : window + start + step, :]
        block32 = block.astype(f32)
        square = jnp.concatenate(halves(block32 * block32), axis=1)
        unit = lax.rsqrt(dot_nt(ones, square)[:1] * (1.0 / width) + epsilon)
        part = slice(start, start + step)
        rate = rate_row[:, part]
        scale = rate * unit
        both = dot_nt(turned2[...], wide(block))
        gate = both[:hidden] * unit
        up = both[hidden:] * unit
        share = sigmoid(gate)
        act = gate * share
        gate_part[:, part] = up * (share + act * (1.0 - share)) * scale
        up_part[:, part] = act * scale
        down_steps[:, part] = (act * up * rate).astype(bf16)


def first_core():
    return lax.rem(lax.axis_index("ctx"), 2) == 0


def key_hidden(window, _, keys, turned2, rate_row, *parts):
    @pl.when(first_core())
    def _fill():
        fill_key_parts(window, keys, turned2, rate_row, *parts)


def own_rows_and_update(
    tile,
    flags,
    down2,
    gain,
    queries,
    highs,
    lows,
    keys,
    values,
    turned2,
    turned,
    down,
    rate_row,
    _gate_part,
    _up_part,
    _down_steps,
    mixed,
    new_gu,
    new_dn,
    gate_part,
    up_part,
    down_steps,
    weights,
    own,
    steps,
    gu,
    dn,
    sems,
):
    rows, width = own.shape
    hidden = down.shape[0]
    window = weights.shape[2] - tile
    total = keys.shape[0] - window
    linked = flags[0] == 1
    length = flags[1]
    head = lax.axis_index("head")
    for t in range(rows // tile):
        start = pl.multiple_of(head * rows + t * tile, tile)
        place = total - rows + t * tile
        span = slice(place, place + tile)
        normed = fast_rows(highs[span, :], lows[span, :], start, length, down2, gain)
        keys_here = keys[pl.ds(start, tile + window), :]
        store_weights(queries[span, :], keys_here, start, length, linked, weights.at[t])
        attended = dot(weights[t], values[pl.ds(start, tile + window), :])
        own[t * tile : (t + 1) * tile, :] = (attended + normed).astype(bf16)
    out_copy = pltpu.make_async_copy(own, mixed.at[0, :, head_columns(head, width)], sems.at[0])
    out_copy.start()
    @pl.when(jnp.logical_not(first_core()))
    def _fill():
        fill_key_parts(window, keys, turned2, rate_row, gate_part, up_part, down_steps)

    step = min(256, total)
    for start in range(0, total, step):
        block_v = values[window + start : window + start + step, :]
        hidden_grad = dot_nt(down2[...], wide(block_v))
        part = slice(start, start + step)
        steps[0:hidden, part] = (hidden_grad * gate_part[:, part]).astype(bf16)
        steps[hidden : 2 * hidden, part] = (hidden_grad * up_part[:, part]).astype(bf16)
    both = dot(steps[...], keys[window:, :])
    for index in range(2):
        part = slice(index * hidden, (index + 1) * hidden)
        gu[index] = renormed(turned[part], both[part], 1).T
    first = pltpu.make_async_copy(gu, new_gu.at[0, 0], sems.at[1])
    first.start()
    dn[...] = renormed(down[...], dot(down_steps[...], values[window:, :]), 0)
    second = pltpu.make_async_copy(dn, new_dn.at[0, 0], sems.at[2])
    second.start()
    out_copy.wait()
    first.wait()
    second.wait()


def place_received(count, *refs):
    got = refs[1:count]
    mixed, sems = refs[count:]
    width = got[0].shape[1]
    head = lax.axis_index("head")
    run_copies(
        [
            (got[s - 1], mixed.at[0, :, head_columns(lax.rem(head + count - s, count), width)])
            for s in range(1, count)
        ],
        sems,
    )


def params():
    return pltpu.CompilerParams(vmem_limit_bytes=24 * 1024 * 1024)


def call(body, name, outs, ins, scratch=(), cost=1, aliases={}):
    spec = {local: in_vmem, in_main: in_hbm, scalars: in_smem}
    return pl.pallas_call(
        body,
        out_shape=[shape for _, shape in outs],
        in_specs=[spec[where] for where, _ in ins],
        out_specs=[spec[where] for where, _ in outs],
        scratch_shapes=list(scratch),
        input_output_aliases=aliases,
        compiler_params=params(),
        cost_estimate=pl.CostEstimate(
            flops=int(cost * 1e6), bytes_accessed=1024, transcendentals=0
        ),
        name=name,
    )(*[where(array) for where, array in ins])


def on_device(
    queries,
    keys,
    values,
    rates,
    tail_keys,
    tail_values,
    state_in_gu,
    state_in_down,
    fresh_gu,
    fresh_down,
    out_gain,
    seq_ids,
    live_lengths,
):
    count = lax.axis_size("head")
    rows = queries.shape[1]
    width = queries.shape[2] // count
    window = tail_keys.shape[0]
    hidden = state_in_down.shape[2]
    total = rows * count
    sent = total - rows
    tile = min(256, rows)
    span = tile + window
    shifts = range(1, count)
    dma = pltpu.SemaphoreType.DMA

    def on_chip(shape, kind):
        return (local, VMEM(shape, kind))

    def in_hbm_out(shape, kind):
        return (in_main, jax.ShapeDtypeStruct(shape, kind))

    def all_local(*arrays):
        return [(local, array) for array in arrays]

    piece = on_chip((rows, width), bf16)

    got_gu = from_behind(state_in_gu[0, 0].reshape(2 * width, hidden), "ctx", 1)
    down_keys, last_v, *packed = call(
        functools.partial(pack, count),
        "pack",
        [on_chip((2 * hidden + window, width), bf16), on_chip((window, width), bf16)]
        + [on_chip((2 * rows, width), bf16)] * (count - 1)
        + [piece] * (count - 1),
        [
            (in_main, array)
            for array in (queries, keys, values, state_in_down, tail_keys, tail_values)
        ],
        scratch=[VMEM((hidden, width), f32), dma((3 * count,))],
    )
    sent_qk, sent_v = packed[: count - 1], packed[count - 1 :]
    got_qk = [from_behind(sent_qk[s - 1], "head", s) for s in shifts]
    got_dk = from_behind(down_keys, "ctx", 1)
    prior_v = from_behind(last_v, "ctx", 1)

    own_q, own_k, own_v, fresh, gain, rate_row, flags = call(
        functools.partial(load, count),
        "load",
        [
            piece,
            piece,
            piece,
            on_chip((3 * width, hidden), f32),
            on_chip((1, width), f32),
            on_chip((1, total), f32),
            (scalars, pltpu.SMEM((2,), jnp.int32)),
        ],
        [
            (in_main, array)
            for array in (
                queries,
                keys,
                values,
                fresh_gu,
                fresh_down,
                out_gain[None],
                rates,
                seq_ids.T,
                live_lengths.T,
            )
        ]
        + all_local(sent_qk[0]),
        scratch=[
            pltpu.SMEM(seq_ids.shape[::-1], jnp.int32),
            pltpu.SMEM(live_lengths.shape[::-1], jnp.int32),
            dma((9 + hidden // width,)),
        ],
    )
    held_v = lax.optimization_barrier((fresh, *sent_v))[1:]
    got_v = [from_behind(held_v[s - 1], "head", s) for s in shifts]
    gate2, up2, turned2, turned, live_rates = call(
        choose_gate_up,
        "choose_gate_up",
        [
            on_chip((2 * width, hidden), bf16),
            on_chip((2 * width, hidden), bf16),
            on_chip((2 * hidden, 2 * width), bf16),
            on_chip((2 * hidden, width), f32),
            on_chip((1, total), f32),
        ],
        [(scalars, flags)] + all_local(got_gu, fresh, rate_row),
        cost=500,
    )
    all_keys_shape = on_chip((window + total, width), bf16)
    all_q, highs, lows, all_keys = call(
        functools.partial(query_hidden, count, tile, window),
        "query_hidden",
        [on_chip((total, width), bf16)]
        + [on_chip((total, hidden), bf16)] * 2
        + [all_keys_shape],
        all_local(gate2, up2, own_q, own_k, *got_qk),
        cost=500,
    )
    down2, down, all_keys = call(
        choose_down,
        "choose_down",
        [on_chip((hidden, 2 * width), bf16), on_chip((hidden, width), f32), all_keys_shape],
        [(scalars, flags)] + all_local(got_dk, fresh, all_keys),
        aliases={3: 2},
    )
    weights, normed = call(
        functools.partial(sent_rows, count, tile),
        "sent_rows",
        [on_chip((sent // tile, tile, span), bf16), on_chip((sent, width), f32)],
        [(scalars, flags)] + all_local(down2, gain, all_keys, all_q, highs, lows),
        cost=1,
    )
    key_parts = [
        on_chip((hidden, total), f32),
        on_chip((hidden, total), f32),
        on_chip((hidden, total), bf16),
    ]
    parts = call(
        functools.partial(key_hidden, window),
        "key_hidden",
        key_parts,
        all_local(normed, all_keys, turned2, live_rates),
    )
    (all_values,) = call(
        start_values,
        "start_values",
        [on_chip((window + total, width), bf16)],
        all_local(parts[2], prior_v, own_v),
        cost=1,
    )
    all_values, *mixed_out = call(
        functools.partial(mix_sent, count),
        "mix_sent",
        [on_chip((window + total, width), bf16)] + [piece] * (count - 1),
        all_local(weights, normed, all_values, *got_v),
        aliases={2: 0},
    )
    mixed_in = [from_behind(mixed_out[s - 1], "head", s) for s in shifts]
    mixed, new_gu, new_down, *_ = call(
        functools.partial(own_rows_and_update, tile),
        "own_rows_and_update",
        [
            in_hbm_out(queries.shape, bf16),
            in_hbm_out(state_in_gu.shape, f32),
            in_hbm_out(state_in_down.shape, f32),
            *key_parts,
        ],
        [(scalars, flags)]
        + all_local(
            down2,
            gain,
            all_q,
            highs,
            lows,
            all_keys,
            all_values,
            turned2,
            turned,
            down,
            live_rates,
            *parts,
        ),
        scratch=[
            VMEM((rows // tile, tile, span), bf16),
            VMEM((rows, width), bf16),
            VMEM((2 * hidden, total), bf16),
            VMEM(state_in_gu.shape[2:], f32),
            VMEM(state_in_down.shape[2:], f32),
            dma((3,)),
        ],
        aliases={12: 3, 13: 4, 14: 5},
    )
    (mixed,) = call(
        functools.partial(place_received, count),
        "place_received",
        [in_hbm_out(queries.shape, bf16)],
        [(in_main, mixed)] + all_local(*mixed_in),
        scratch=[dma((count - 1,))],
        aliases={0: 0},
    )
    return (mixed, new_gu, new_down)


def solution(mesh):
    placed = (
        P(None, ("ctx", "head"), None),
        P(None, ("ctx", "head"), None),
        P(None, ("ctx", "head"), None),
        P(None, "head", "ctx"),
        P("ctx", "head"),
        P("ctx", "head"),
        P("ctx", "head", None, None, None),
        P("ctx", "head", None, None),
        P("head", None, None, None),
        P("head", None, None),
        P("head"),
        P(),
        P(),
    )
    return jax.shard_map(
        on_device,
        mesh=mesh,
        in_specs=placed,
        out_specs=(
            P(None, ("ctx", "head"), None),
            P("ctx", "head", None, None, None),
            P("ctx", "head", None, None),
        ),
        check_vma=False,
    )
```

```python
import functools
import math

import jax
import jax.numpy as jnp
from jax import lax
from jax.experimental import pallas as pl
from jax.experimental.pallas import tpu as pltpu
from jax.sharding import PartitionSpec as P

epsilon = 1e-06
masked = -1e30
f32 = jnp.float32
bf16 = jnp.bfloat16

VMEM = pltpu.VMEM
in_vmem = pl.BlockSpec(memory_space=pltpu.VMEM)
in_smem = pl.BlockSpec(memory_space=pltpu.SMEM)
in_hbm = pl.BlockSpec(memory_space=pltpu.HBM)


def from_behind(shard, axis, by):
    size = lax.axis_size(axis)
    return lax.ppermute(shard, axis, [(i, (i + by) % size) for i in range(size)])


def local(array):
    return pltpu.with_memory_space_constraint(array, pltpu.VMEM)


def in_main(array):
    return pltpu.with_memory_space_constraint(array, pltpu.HBM)


def scalars(array):
    return pltpu.with_memory_space_constraint(array, pltpu.SMEM)


def run_copies(pairs, sems):
    copies = [
        pltpu.make_async_copy(source, target, sems.at[i]) for i, (source, target) in enumerate(pairs)
    ]
    for copy in copies:
        copy.start()
    for copy in copies:
        copy.wait()


def head_columns(index, width):
    return pl.ds(pl.multiple_of(index * width, width), width)


def wide(array):
    return jnp.concatenate([array, array], axis=1)


def halves(array):
    high = array.astype(bf16)
    low = (array - high.astype(f32)).astype(bf16)
    return high, low


def dot(left, right):
    return jnp.dot(left, right, preferred_element_type=f32)


def dot_nt(left, right):
    return lax.dot_general(left, right, (((1,), (1,)), ((), ())), preferred_element_type=f32)


def sigmoid(x):
    return 0.5 * jnp.tanh(0.5 * x) + 0.5


def row_block(index, rows):
    return pl.ds(pl.multiple_of(index * rows, rows), rows)


def fast_rows(high, low, first_row, length, down2, gain):
    count = high.shape[0]
    width = down2.shape[1] // 2
    both = dot(high, down2[...])
    fast = both[:, :width] + both[:, width:] + dot(low, down2[:, :width])
    scale = lax.rsqrt(jnp.mean(fast * fast, axis=-1, keepdims=True) + epsilon)
    row = first_row + lax.broadcasted_iota(jnp.int32, (count, 1), 0)
    return fast * jnp.where(row < length, scale, 0.0) * gain[...]


def store_weights(queries, keys, first_row, length, linked, out):
    tile, width = queries.shape
    window = keys.shape[0] - tile
    place = first_row - window + lax.broadcasted_iota(jnp.int32, (1, tile + window), 1)
    bias = jnp.where((place < length) & ((place >= 0) | linked), 0.0, masked)
    row = lax.broadcasted_iota(jnp.int32, (tile, tile), 0)
    column = lax.broadcasted_iota(jnp.int32, (tile, tile), 1)
    later = column > row
    factor = math.log2(math.e) / math.sqrt(width)
    scores = dot_nt(queries, keys) * factor
    first = jnp.where(later, scores[:, :tile] + bias[:, :tile], masked)
    last = scores[:, window:]
    last = jnp.where(column == row, last, last + bias[:, window:])
    last = jnp.where(later, masked, last)
    parts = [(0, first), (window, last)]
    if tile < window:
        parts.append((tile, scores[:, tile:window] + bias[:, tile:window]))
    largest = functools.reduce(
        jnp.maximum, [jnp.max(part, axis=-1, keepdims=True) for _, part in parts]
    )
    parts = [(offset, jnp.exp2(part - largest)) for offset, part in parts]
    total = sum(jnp.sum(part, axis=-1, keepdims=True) for _, part in parts)
    token = first_row + lax.broadcasted_iota(jnp.int32, (tile, 1), 0)
    scale = jnp.where(token < length, 1.0 / total, 0.0)
    for offset, part in parts:
        out[:, offset : offset + part.shape[1]] = (part * scale).astype(bf16)


def join(count, window, own, got, joined):
    rows = own.shape[0]
    head = lax.axis_index("head")
    joined[pl.ds(pl.multiple_of(window + head * rows, rows), rows), :] = own[...]
    for s in range(1, count):
        source = lax.rem(head + count - s, count)
        joined[pl.ds(pl.multiple_of(window + source * rows, rows), rows), :] = got[s - 1][...]


def pack(count, q_ref, k_ref, v_ref, dn_ref, tail_k, tail_v, *refs):
    down_keys, last_v = refs[:2]
    sent_qk, sent_v = refs[2 : 1 + count], refs[1 + count : 2 * count]
    down, sems = refs[-2:]
    head = lax.axis_index("head")
    hidden, width = down.shape
    rows = sent_v[0].shape[0]
    pairs = [(dn_ref.at[0, 0], down)]
    for s in range(1, count):
        columns = head_columns(lax.rem(head + s, count), width)
        pairs.append((q_ref.at[0, :, columns], sent_qk[s - 1].at[0:rows]))
        pairs.append((k_ref.at[0, :, columns], sent_qk[s - 1].at[rows : 2 * rows]))
        pairs.append((v_ref.at[0, :, columns], sent_v[s - 1]))
    pairs += [(tail_k, down_keys.at[2 * hidden :]), (tail_v, last_v)]
    run_copies(pairs, sems)
    high, low = halves(down[...])
    down_keys[0:hidden] = high
    down_keys[hidden : 2 * hidden] = low


def load(
    count, q_ref, k_ref, v_ref, fresh_gu, fresh_dn, gain, rates, ids_ref, len_ref, _, own_q, own_k,
    own_v, fresh,
    gain_row, rate_row, flags, ids, lens, sems
):
    head = lax.axis_index("head")
    here = lax.axis_index("ctx")
    width = own_k.shape[1]
    columns = head_columns(head, width)
    pairs = [
        (q_ref.at[0, :, columns], own_q),
        (k_ref.at[0, :, columns], own_k),
        (v_ref.at[0, :, columns], own_v),
        (fresh_gu.at[0, 0], fresh.at[0:width]),
        (fresh_gu.at[0, 1], fresh.at[width : 2 * width]),
    ]
    for group in range(fresh_dn.shape[1] // width):
        part = slice(group * width, (group + 1) * width)
        pairs.append((fresh_dn.at[0, part], fresh.at[2 * width : 3 * width, part]))
    pairs += [(gain, gain_row), (rates.at[0], rate_row), (ids_ref, ids), (len_ref, lens)]
    run_copies(pairs, sems)
    size = ids.shape[1]
    before = lax.rem(here + size - 1, size)
    flags[0] = (ids[1, here] == ids[0, before]).astype(jnp.int32)
    flags[1] = lens[0, here]


def hidden_rows(queries, gate2, up2):
    queries32 = queries.astype(f32)
    unit = lax.rsqrt(jnp.mean(queries32 * queries32, axis=-1, keepdims=True) + epsilon)
    doubled = wide(queries)
    gate = dot(doubled, gate2[...]) * unit
    up = dot(doubled, up2[...]) * unit
    return halves(gate * sigmoid(gate) * up)


def query_hidden(count, tile, window, gate2, up2, own_q, own_k, *refs):
    got_qk, (queries, highs, lows, keys) = refs[: count - 1], refs[count - 1 :]
    rows, width = own_k.shape
    for s in range(1, count + 1):
        source = own_q if s == count else got_qk[count - s - 1]
        for t in range(rows // tile):
            span = slice((s - 1) * rows + t * tile, (s - 1) * rows + (t + 1) * tile)
            block = source[t * tile : (t + 1) * tile, :]
            queries[span, :] = block
            high, low = hidden_rows(block, gate2, up2)
            highs[span, :] = high
            lows[span, :] = low
    join(count, window, own_k, [got.at[rows : 2 * rows] for got in got_qk], keys)


def choose_gate_up(flags, got_gu, fresh, rates, gate2, up2, turned2, turned, rate_row):
    hidden = fresh.shape[1]
    width = got_gu.shape[0] // 2
    linked = flags[0] == 1
    length = flags[1]
    for index, split in enumerate((gate2, up2)):
        rows = slice(index * width, (index + 1) * width)
        weight = jnp.where(linked, got_gu[rows], fresh[rows])
        split[...] = jnp.concatenate(halves(weight), axis=0)
        part = slice(index * hidden, (index + 1) * hidden)
        weight = weight.T
        turned[part] = weight
        turned2[part] = jnp.concatenate(halves(weight), axis=1)
    token = lax.broadcasted_iota(jnp.int32, rates.shape, 1)
    rate_row[...] = jnp.where(token < length, -rates[...], 0.0)


def choose_down(flags, down_keys, fresh, keys, down2, down, joined):
    hidden, width = down.shape
    window = down_keys.shape[0] - 2 * hidden
    linked = flags[0] == 1
    fresh_down = jnp.concatenate(
        [fresh[2 * width :, g * width : (g + 1) * width] for g in range(hidden // width)], axis=0
    )
    got_down = down_keys[0:hidden].astype(f32) + down_keys[hidden : 2 * hidden].astype(f32)
    w_down = jnp.where(linked, got_down, fresh_down)
    down[...] = w_down
    down2[...] = jnp.concatenate(halves(w_down), axis=1)
    joined[0:window] = down_keys[2 * hidden :]


def sent_rows(count, tile, flags, down2, gain, keys, queries, highs, lows, weights, normed):
    rows = queries.shape[0] // count
    window = keys.shape[0] - count * rows
    linked = flags[0] == 1
    length = flags[1]
    head = lax.axis_index("head")
    for s in range(1, count):
        device = lax.rem(head + s, count)
        for t in range(rows // tile):
            place = (s - 1) * rows + t * tile
            start = pl.multiple_of(device * rows + t * tile, tile)
            span = slice(place, place + tile)
            normed[span, :] = fast_rows(highs[span, :], lows[span, :], start, length, down2, gain)
            store_weights(
                queries[span, :],
                keys[pl.ds(start, tile + window), :],
                start,
                length,
                linked,
                weights.at[place // tile],
            )


def start_values(_, tail_v, own_v, values):
    window = tail_v.shape[0]
    values[0:window, :] = tail_v[...]
    join(1, window, own_v, [], values)


def mix_sent(count, weights, normed, _, *refs):
    got_v, values, outs = refs[: count - 1], refs[count - 1], refs[count:]
    rows = got_v[0].shape[0]
    tile, span = weights.shape[1:]
    head = lax.axis_index("head")
    for s in range(1, count):
        source = lax.rem(head + count - s, count)
        start = span - tile + source * rows
        values[pl.ds(pl.multiple_of(start, rows), rows), :] = got_v[s - 1][...]
    for s in range(1, count):
        device = lax.rem(head + s, count)
        for t in range(rows // tile):
            place = (s - 1) * rows + t * tile
            start = pl.multiple_of(device * rows + t * tile, tile)
            attended = dot(weights[place // tile], values[pl.ds(start, span), :])
            outs[s - 1][t * tile : (t + 1) * tile, :] = (
                attended + normed[place : place + tile, :]
            ).astype(bf16)


def renormed(old_weight, gradient, axis):
    new_weight = old_weight - gradient
    old_square = jnp.mean(old_weight * old_weight, axis=axis, keepdims=True) + epsilon
    new_square = jnp.mean(new_weight * new_weight, axis=axis, keepdims=True) + epsilon
    return new_weight * (jnp.sqrt(old_square) / jnp.sqrt(new_square))


def own_rows_and_update(
    tile,
    flags,
    down2,
    gain,
    queries,
    highs,
    lows,
    keys,
    values,
    turned2,
    turned,
    down,
    rate_row,
    own,
    new_gu,
    new_dn,
    weights,
    steps,
    gu,
    dn,
    sems,
):
    rows, width = own.shape
    hidden = down.shape[0]
    window = weights.shape[2] - tile
    total = keys.shape[0] - window
    linked = flags[0] == 1
    length = flags[1]
    head = lax.axis_index("head")
    ones = jnp.ones((8, 2 * width), bf16)
    step = min(256, total)
    for start in range(0, total, step):
        block_k = keys[window + start : window + start + step, :]
        block_v = values[window + start : window + start + step, :]
        block32 = block_k.astype(f32)
        square = jnp.concatenate(halves(block32 * block32), axis=1)
        unit = lax.rsqrt(dot_nt(ones, square)[:1] * (1.0 / width) + epsilon)
        rate = rate_row[:, start : start + step]
        both = dot_nt(turned2[...], wide(block_k))
        gate = both[:hidden] * unit
        up = both[hidden:] * unit
        share = sigmoid(gate)
        act = gate * share
        hidden_grad = dot_nt(down2[...], wide(block_v)) * (rate * unit)
        part = slice(start, start + step)
        steps[0:hidden, part] = (hidden_grad * up * (share + act * (1.0 - share))).astype(bf16)
        steps[hidden : 2 * hidden, part] = (hidden_grad * act).astype(bf16)
        steps[2 * hidden : 3 * hidden, part] = (act * up * rate).astype(bf16)
    both = dot(steps[0 : 2 * hidden, :], keys[window:, :])
    for index in range(2):
        part = slice(index * hidden, (index + 1) * hidden)
        gu[index] = renormed(turned[part], both[part], 1).T
    first = pltpu.make_async_copy(gu, new_gu.at[0, 0], sems.at[0])
    first.start()
    dn[...] = renormed(down[...], dot(steps[2 * hidden :, :], values[window:, :]), 0)
    second = pltpu.make_async_copy(dn, new_dn.at[0, 0], sems.at[1])
    second.start()
    for t in range(rows // tile):
        start = pl.multiple_of(head * rows + t * tile, tile)
        place = total - rows + t * tile
        span = slice(place, place + tile)
        normed = fast_rows(highs[span, :], lows[span, :], start, length, down2, gain)
        keys_here = keys[pl.ds(start, tile + window), :]
        store_weights(queries[span, :], keys_here, start, length, linked, weights.at[t])
        attended = dot(weights[t], values[pl.ds(start, tile + window), :])
        own[t * tile : (t + 1) * tile, :] = (attended + normed).astype(bf16)
    first.wait()
    second.wait()


def place(count, *refs):
    parts, (mixed, sems) = refs[:count], refs[count:]
    width = parts[0].shape[1]
    head = lax.axis_index("head")
    run_copies(
        [
            (parts[s], mixed.at[0, :, head_columns(lax.rem(head + count - s, count), width)])
            for s in range(count)
        ],
        sems,
    )


def params():
    return pltpu.CompilerParams(vmem_limit_bytes=24 * 1024 * 1024)


def call(body, name, outs, ins, scratch=(), cost=1, aliases={}):
    spec = {local: in_vmem, in_main: in_hbm, scalars: in_smem}
    return pl.pallas_call(
        body,
        out_shape=[shape for _, shape in outs],
        in_specs=[spec[where] for where, _ in ins],
        out_specs=[spec[where] for where, _ in outs],
        scratch_shapes=list(scratch),
        input_output_aliases=aliases,
        compiler_params=params(),
        cost_estimate=pl.CostEstimate(
            flops=int(cost * 1e6), bytes_accessed=1024, transcendentals=0
        ),
        name=name,
    )(*[where(array) for where, array in ins])


def on_device(
    queries,
    keys,
    values,
    rates,
    tail_keys,
    tail_values,
    state_in_gu,
    state_in_down,
    fresh_gu,
    fresh_down,
    out_gain,
    seq_ids,
    live_lengths,
):
    count = lax.axis_size("head")
    rows = queries.shape[1]
    width = queries.shape[2] // count
    window = tail_keys.shape[0]
    hidden = state_in_down.shape[2]
    total = rows * count
    sent = total - rows
    tile = min(256, rows)
    span = tile + window
    shifts = range(1, count)
    dma = pltpu.SemaphoreType.DMA

    def on_chip(shape, kind):
        return (local, VMEM(shape, kind))

    def in_hbm_out(shape, kind):
        return (in_main, jax.ShapeDtypeStruct(shape, kind))

    def all_local(*arrays):
        return [(local, array) for array in arrays]

    piece = on_chip((rows, width), bf16)

    got_gu = from_behind(state_in_gu[0, 0].reshape(2 * width, hidden), "ctx", 1)
    down_keys, last_v, *packed = call(
        functools.partial(pack, count),
        "pack",
        [on_chip((2 * hidden + window, width), bf16), on_chip((window, width), bf16)]
        + [on_chip((2 * rows, width), bf16)] * (count - 1)
        + [piece] * (count - 1),
        [
            (in_main, array)
            for array in (queries, keys, values, state_in_down, tail_keys, tail_values)
        ],
        scratch=[VMEM((hidden, width), f32), dma((3 * count,))],
    )
    sent_qk, sent_v = packed[: count - 1], packed[count - 1 :]
    got_qk = [from_behind(sent_qk[s - 1], "head", s) for s in shifts]
    got_dk = from_behind(down_keys, "ctx", 1)
    prior_v = from_behind(last_v, "ctx", 1)

    own_q, own_k, own_v, fresh, gain, rate_row, flags = call(
        functools.partial(load, count),
        "load",
        [
            piece,
            piece,
            piece,
            on_chip((3 * width, hidden), f32),
            on_chip((1, width), f32),
            on_chip((1, total), f32),
            (scalars, pltpu.SMEM((2,), jnp.int32)),
        ],
        [
            (in_main, array)
            for array in (
                queries,
                keys,
                values,
                fresh_gu,
                fresh_down,
                out_gain[None],
                rates,
                seq_ids.T,
                live_lengths.T,
            )
        ]
        + all_local(sent_qk[0]),
        scratch=[
            pltpu.SMEM(seq_ids.shape[::-1], jnp.int32),
            pltpu.SMEM(live_lengths.shape[::-1], jnp.int32),
            dma((9 + hidden // width,)),
        ],
    )
    held_v = lax.optimization_barrier((fresh, *sent_v))[1:]
    got_v = [from_behind(held_v[s - 1], "head", s) for s in shifts]
    gate2, up2, turned2, turned, live_rates = call(
        choose_gate_up,
        "choose_gate_up",
        [
            on_chip((2 * width, hidden), bf16),
            on_chip((2 * width, hidden), bf16),
            on_chip((2 * hidden, 2 * width), bf16),
            on_chip((2 * hidden, width), f32),
            on_chip((1, total), f32),
        ],
        [(scalars, flags)] + all_local(got_gu, fresh, rate_row),
        cost=500,
    )
    all_keys_shape = on_chip((window + total, width), bf16)
    all_q, highs, lows, all_keys = call(
        functools.partial(query_hidden, count, tile, window),
        "query_hidden",
        [on_chip((total, width), bf16)]
        + [on_chip((total, hidden), bf16)] * 2
        + [all_keys_shape],
        all_local(gate2, up2, own_q, own_k, *got_qk),
        cost=500,
    )
    down2, down, all_keys = call(
        choose_down,
        "choose_down",
        [on_chip((hidden, 2 * width), bf16), on_chip((hidden, width), f32), all_keys_shape],
        [(scalars, flags)] + all_local(got_dk, fresh, all_keys),
        aliases={3: 2},
    )
    weights, normed = call(
        functools.partial(sent_rows, count, tile),
        "sent_rows",
        [on_chip((sent // tile, tile, span), bf16), on_chip((sent, width), f32)],
        [(scalars, flags)] + all_local(down2, gain, all_keys, all_q, highs, lows),
        cost=1,
    )
    (all_values,) = call(
        start_values,
        "start_values",
        [on_chip((window + total, width), bf16)],
        all_local(normed, prior_v, own_v),
        cost=1,
    )
    all_values, *mixed_out = call(
        functools.partial(mix_sent, count),
        "mix_sent",
        [on_chip((window + total, width), bf16)] + [piece] * (count - 1),
        all_local(weights, normed, all_values, *got_v),
        aliases={2: 0},
    )
    mixed_in = [from_behind(mixed_out[s - 1], "head", s) for s in shifts]
    mixed_own, new_gu, new_down = call(
        functools.partial(own_rows_and_update, tile),
        "own_rows_and_update",
        [
            piece,
            in_hbm_out(state_in_gu.shape, f32),
            in_hbm_out(state_in_down.shape, f32),
        ],
        [(scalars, flags)]
        + all_local(
            down2,
            gain,
            all_q,
            highs,
            lows,
            all_keys,
            all_values,
            turned2,
            turned,
            down,
            live_rates,
        ),
        scratch=[
            VMEM((rows // tile, tile, span), bf16),
            VMEM((3 * hidden, total), bf16),
            VMEM(state_in_gu.shape[2:], f32),
            VMEM(state_in_down.shape[2:], f32),
            dma((2,)),
        ],
    )
    (mixed,) = call(
        functools.partial(place, count),
        "place_received",
        [in_hbm_out(queries.shape, bf16)],
        all_local(mixed_own, *mixed_in),
        scratch=[dma((count,))],
    )
    return (mixed, new_gu, new_down)


def solution(mesh):
    placed = (
        P(None, ("ctx", "head"), None),
        P(None, ("ctx", "head"), None),
        P(None, ("ctx", "head"), None),
        P(None, "head", "ctx"),
        P("ctx", "head"),
        P("ctx", "head"),
        P("ctx", "head", None, None, None),
        P("ctx", "head", None, None),
        P("head", None, None, None),
        P("head", None, None),
        P("head"),
        P(),
        P(),
    )
    return jax.shard_map(
        on_device,
        mesh=mesh,
        in_specs=placed,
        out_specs=(
            P(None, ("ctx", "head"), None),
            P("ctx", "head", None, None, None),
            P("ctx", "head", None, None),
        ),
        check_vma=False,
    )
```
